32 devices in a mesh: dp: 4 (over x, core), expert: 8 (over z, y).
Axes of the slice: x: 2, y: 2, z: 4, core: 2. Of those that a mesh axis runs over, the one named last changes fastest.
Arguments:
- grad_out: bfloat16 [4096, 3584], P(('dp', 'expert')), may hold values from -1.5 to 1.5
- gate_probs: float32 [4096, 4], P(('dp', 'expert')), may hold values from 0.05 to 0.3
- expert_route: int32 [4096, 4], P(('dp', 'expert')), may hold values from 0 to 11, all different within a row; in each aligned block of 128 rows (0 to 127, 128 to 255, ...) at most 48 rows name the same one
- replica_pick: int32 [4096, 4], P(('dp', 'expert')), may hold values from 0 to 59
- slot_expert: int32 [16], replicated, may hold values from 0 to 11, as said below
- saved_hidden: bfloat16 [4, 8, 8, 2, 48, 1024], P('dp', 'expert'), may hold values from -6 to 6
- master: float32 [16, 1024, 3584], P('expert', 'dp'), as said below
- first_moment: bfloat16 [16, 1024, 3584], P('expert', 'dp'), as said below
- second_moment: bfloat16 [16, 1024, 3584], P('expert', 'dp'), as said below
Outputs:
- hidden_grad: bfloat16 [4, 8, 8, 2, 48, 1024], P('dp', 'expert')
- gate_grad: float32 [4096, 4], P(('dp', 'expert'))
- new_master: float32 [16, 1024, 3584], P('expert', 'dp')
- new_first: bfloat16 [16, 1024, 3584], P('expert', 'dp')
- new_second: bfloat16 [16, 1024, 3584], P('expert', 'dp')
The draws below stay inside these ranges and needn't reach their ends.
Inputs may be any that keep to these rules, and one draw needn't show every extreme that they name: `expert_route`: each row names 4 different experts; in the rows of one device no expert is named more than 48 times, a bound that some block reaches. `slot_expert`: every expert has at least one slot; experts 0 to 2 have two or more slots each, every other expert exactly one. `master`: slots holding the same expert hold equal values. `first_moment`: slots holding the same expert hold equal values. `second_moment`: slots holding the same expert hold equal values; all entries are positive.
All inputs are finite; a program needn't handle non-finite values.
Results may differ from the reference program's by a relative error of at most 0.017.
Values may be sent and summed in bfloat16 or wider, within the bound.
No kernel may reach another device: no remote copies, remote signals or barrier semaphores. Data moves between devices by JAX's collectives and lax.ppermute only.
A program may use at most 128 MiB of HBM per device.

```python
import math
import jax
import jax.numpy as jnp
import numpy as np
from jax import lax

D = 3584
HID = 1024
TOPK = 4
HOT = 3
TOK_DEV = 128
SLOT_DEV = 2
N_SLOTS = 16
REPLICAS = 4
EXPERTS = 12
CAP = 48
TOKENS = 4096
N_DP = 4
N_EXPERT = 8


def placement_table(key):
    base_key = jax.random.fold_in(key, 11)
    extra_key = jax.random.fold_in(base_key, 1)
    order_key = jax.random.fold_in(base_key, 2)
    start_key = jax.random.fold_in(base_key, 3)
    start = jax.random.randint(start_key, (), 0, N_EXPERT).astype(jnp.int32)
    first_pos = start * SLOT_DEV
    second_pos = (start + 1) % N_EXPERT * SLOT_DEV
    third_pos = (start + N_EXPERT // 2) % N_EXPERT * SLOT_DEV
    extra = jax.random.randint(extra_key, (REPLICAS - HOT - 1,), 0, HOT).astype(jnp.int32)
    listed = jnp.concatenate([jnp.arange(1, EXPERTS, dtype=jnp.int32), jnp.arange(1, HOT, dtype=jnp.int32), extra])
    order = jax.random.permutation(order_key, N_SLOTS - 3)
    rest = listed[order].astype(jnp.int32)
    slot_ids = jnp.arange(N_SLOTS, dtype=jnp.int32)
    fixed = (slot_ids == first_pos) | (slot_ids == second_pos) | (slot_ids == third_pos)
    free_order = jnp.argsort(fixed.astype(jnp.int32), stable=True).astype(jnp.int32)
    table = jnp.zeros((N_SLOTS,), jnp.int32).at[free_order[:N_SLOTS - 3]].set(rest)
    return table.astype(jnp.int32)


def draw_slot_expert(key, part):
    return placement_table(key)


def draw_master(key, part):
    table = placement_table(key)
    value_key = jax.random.fold_in(key, 21)
    values = jax.random.normal(value_key, (EXPERTS, HID, D), jnp.float32) * D ** (-0.5)
    return values[table]


def draw_first_moment(key, part):
    table = placement_table(key)
    value_key = jax.random.fold_in(key, 22)
    values = jax.random.normal(value_key, (EXPERTS, HID, D), jnp.float32) * 0.3
    return values[table].astype(jnp.bfloat16)


def draw_second_moment(key, part):
    table = placement_table(key)
    value_key = jax.random.fold_in(key, 23)
    values = jnp.exp(jax.random.uniform(value_key, (EXPERTS, HID, D), jnp.float32, -2.3, 1.4))
    return values[table].astype(jnp.bfloat16)


def plant(entries, rng, least, high):
    longest = entries.shape.index(max(entries.shape))
    spots = []
    for shift in (0, 1):
        where = [jax.random.randint(jax.random.fold_in(rng, axis), (), 0, length) for axis, length in enumerate(entries.shape)]
        where[longest] = (where[longest] + shift) % entries.shape[longest]
        spots.append(tuple(where))
    return entries.at[spots[0]].set(least).at[spots[1]].set(high)


def levels(key, dims, split, low, largest):
    def one(axis_at, parts):
        draws = jax.random.uniform(jax.random.fold_in(jax.random.fold_in(key, 6), axis_at), (parts,), jnp.float32, low / len(split), largest / len(split))
        return jnp.repeat(jnp.exp(draws), dims[axis_at] // parts).reshape((-1,) + (1,) * (len(dims) - axis_at - 1))

    factor_of = one(*split[0])
    for cut in split[1:]:
        factor_of = factor_of * one(*cut)
    return factor_of


def shared_out(key, own, number, rows, number_of, top, bound, slope):
    sequence = jax.random.permutation(key, number_of)
    packed, usual = portions_of(number_of, rows * top, bound, slope, True), portions_of(number_of, rows * top, bound, slope, False)
    places = jnp.arange(number_of)

    def named(sizes, turn):
        used = int((sizes > 0).sum())
        fixed = max(1, used // 4)
        passed = fixed + (places - fixed + turn * (used - fixed)) % max(1, number_of - fixed)
        return jnp.zeros((number_of,), jnp.int32).at[sequence[jnp.where(places < fixed, places, passed)]].set(jnp.asarray(sizes, jnp.int32))

    sizes = jnp.where(number % 4 == 0, named(packed, number // 4), named(usual, number - number // 4 - 1))
    mixed = jax.random.permutation(jax.random.fold_in(own, 3), number_of)
    donor, receiver = mixed[0:number_of // 2 * 2:2], mixed[1:number_of // 2 * 2:2]
    margin = jnp.minimum(sizes[donor] - 1, bound - sizes[receiver]) // 2
    margin = jnp.where((donor == sequence[0]) | (receiver == sequence[0]) | (sizes[receiver] == 0), 0, jnp.maximum(margin, 0))
    passed = jax.random.randint(jax.random.fold_in(own, 4), (number_of // 2,), 0, 1 << 20) % (margin + 1)
    sizes = sizes.at[donor].add(-passed).at[receiver].add(passed)
    members = jnp.searchsorted(jnp.cumsum(sizes), jnp.arange(rows * top), side="right").astype(jnp.int32)
    table = members.reshape(top, rows).T
    table = table[jax.random.permutation(jax.random.fold_in(own, 1), rows)]
    turn = jax.random.randint(jax.random.fold_in(own, 2), (rows, 1), 0, top)
    return jnp.take_along_axis(table, (jnp.arange(top)[None, :] + turn) % top, axis=1)


def portions_of(number_of, total, bound, lean, full):
    weights = [(1 << 20) // math.isqrt(standing ** lean) + 1 for standing in range(1, number_of + 1)]
    largest = bound if full else min(bound, max(-(-total // number_of), total * weights[0] // sum(weights)))
    least = 1 if total - largest >= number_of - 1 else 0
    given, spare = [largest] + [least] * (number_of - 1), total - largest - least * (number_of - 1)
    while spare > 0:
        candidates = [i for i in range(1, number_of) if given[i] < largest] or [i for i in range(1, number_of) if given[i] < bound]
        pool, budget = sum([weights[i] for i in candidates]), spare
        for i in candidates:
            more = min(bound - given[i], max(1, budget * weights[i] // pool), spare)
            given[i] = given[i] + more
            spare = spare - more
    return np.array(given)


def gaussian(stream_key, extent, spread, reach, pieces=(), held_as=jnp.bfloat16):
    array = jax.random.normal(stream_key, extent, jnp.float32) * spread
    if len(pieces) > 0:
        array = levels(stream_key, extent, pieces, -0.22, 0.18) * array
    return jnp.clip(array, min=-reach, max=reach).astype(held_as)


def setup_inputs(seed: int = 0) -> dict:
    arg_keys = jax.random.split(jax.random.key(seed), 10)
    grad_out = gaussian(arg_keys[0], (TOKENS, D), 0.25, 1.5, ((0, 32),))
    gate_probs = jnp.clip(0.05 + 0.25 * jax.random.uniform(arg_keys[1], (TOKENS, TOPK), jnp.float32) ** levels(arg_keys[1], (TOKENS, TOPK), ((0, 32),), -0.2, 0.2), 0.05, 0.3)
    expert_route_keys = jax.random.split(jax.random.fold_in(arg_keys[2], 1), TOKENS // TOK_DEV)
    expert_route_turns = jax.random.permutation(jax.random.fold_in(arg_keys[2], 3), TOKENS // TOK_DEV)
    expert_route = jax.vmap(lambda own, number: shared_out(jax.random.fold_in(arg_keys[2], 2), own, number, TOK_DEV, EXPERTS, TOPK, CAP, 1))(expert_route_keys, expert_route_turns).reshape((TOKENS, TOPK))
    replica_pick = plant(jax.random.randint(arg_keys[3], (TOKENS, TOPK), 0, 60), jax.random.fold_in(arg_keys[3], 1), 0, 59).astype(jnp.int32)
    slot_expert = draw_slot_expert(jax.random.fold_in(arg_keys[9], 71), 0)
    saved_hidden = gaussian(arg_keys[5], (N_DP, N_EXPERT, N_EXPERT, SLOT_DEV, CAP, HID), 1.0, 6.0, ((0, 4), (1, 8)))
    master = draw_master(jax.random.fold_in(arg_keys[9], 71), 0)
    first_moment = draw_first_moment(jax.random.fold_in(arg_keys[9], 71), 0)
    second_moment = draw_second_moment(jax.random.fold_in(arg_keys[9], 71), 0)
    return {"grad_out": grad_out, "gate_probs": gate_probs, "expert_route": expert_route, "replica_pick": replica_pick, "slot_expert": slot_expert, "saved_hidden": saved_hidden, "master": master, "first_moment": first_moment, "second_moment": second_moment}


beta_one = 0.9
beta_two = 0.95
learn_rate = 0.00022
decay_rate = 0.1
epsilon = 1e-08
correct_one = 0.6513215599
correct_two = 0.4012630607

def reference(grad_out, gate_probs, expert_route, replica_pick, slot_expert, saved_hidden, master, first_moment, second_moment):
    dp_count, dev_count, _, slot_dev, capacity, hidden_count = saved_hidden.shape
    slot_count = slot_expert.shape[0]
    feature_count = grad_out.shape[1]
    top_count = gate_probs.shape[1]
    tok_rows = grad_out.shape[0] // (dp_count * dev_count)
    assigned = tok_rows * top_count
    slot_ids = jnp.arange(slot_count, dtype=jnp.int32)
    same_expert = slot_expert[:, None] == slot_expert[None, :]
    slot_rank = lax.optimization_barrier(jnp.sum(same_expert & (slot_ids[None, :] < slot_ids[:, None]), axis=1)).astype(jnp.int32)
    experts = expert_route.reshape(dp_count, dev_count, assigned)
    replica_picks = replica_pick.reshape(dp_count, dev_count, assigned)
    host_mask = slot_expert[None, None, None, :] == experts[..., None]
    copy_count = lax.optimization_barrier(jnp.sum(host_mask.astype(jnp.int32), axis=-1)).astype(jnp.int32)
    chosen = host_mask & (slot_rank[None, None, None, :] == (replica_picks % copy_count)[..., None])
    target = lax.optimization_barrier(jnp.sum(jnp.where(chosen, slot_ids, 0), axis=-1)).astype(jnp.int32)
    onehot = (target[..., None] == slot_ids).astype(jnp.int32)
    before = jnp.cumsum(onehot, axis=2) - onehot
    position = lax.optimization_barrier(jnp.sum(onehot * before, axis=-1)).astype(jnp.int32)
    dp_grid = jnp.broadcast_to(jnp.arange(dp_count, dtype=jnp.int32)[:, None, None], target.shape)
    dev_grid = jnp.broadcast_to(jnp.arange(dev_count, dtype=jnp.int32)[None, :, None], target.shape)
    row_grid = jnp.broadcast_to(jnp.arange(assigned, dtype=jnp.int32)[None, None, :], target.shape)
    lookup = jnp.full((dp_count, slot_count, dev_count, capacity), -1, jnp.int32)
    lookup = lookup.at[dp_grid, target, dev_grid, position].set(row_grid)
    token_grads = grad_out.reshape(dp_count, dev_count, tok_rows, feature_count)
    gate_values = gate_probs.astype(jnp.bfloat16).reshape(dp_count, dev_count, assigned)
    dp_index = jnp.arange(dp_count, dtype=jnp.int32)[:, None, None]
    dev_index = jnp.arange(dev_count, dtype=jnp.int32)[None, :, None]

    def per_slot(slot_id):
        row_ids = lax.dynamic_index_in_dim(lookup, slot_id, axis=1, keepdims=False)
        live_rows = row_ids >= 0
        safe_rows = jnp.maximum(row_ids, 0)
        picked = token_grads[dp_index, dev_index, safe_rows // top_count]
        bf_zero = jnp.zeros((), jnp.bfloat16)
        dispatched = jnp.where(live_rows[..., None], picked, bf_zero)
        gate_rows = jnp.where(live_rows, gate_values[dp_index, dev_index, safe_rows], bf_zero)
        device_part = lax.dynamic_index_in_dim(saved_hidden, slot_id // slot_dev, axis=1, keepdims=False)
        hidden = lax.dynamic_index_in_dim(device_part, slot_id % slot_dev, axis=2, keepdims=False)
        weight = lax.dynamic_index_in_dim(master, slot_id, axis=0, keepdims=False).astype(jnp.bfloat16)
        projected = jnp.einsum('pqcd,hd->pqch', dispatched.astype(jnp.float32), weight.astype(jnp.float32))
        gate_scale = gate_rows.astype(jnp.float32)[..., None]
        hidden_grad = (gate_scale * projected).astype(jnp.bfloat16)
        gate_terms = lax.optimization_barrier(jnp.sum(hidden.astype(jnp.float32) * projected, axis=-1))
        scaled = (gate_scale * dispatched.astype(jnp.float32)).astype(jnp.bfloat16)
        partial_value = jnp.einsum('pqch,pqcd->phd', hidden.astype(jnp.float32), scaled.astype(jnp.float32))
        rounded = lax.optimization_barrier(partial_value.astype(jnp.bfloat16))
        summed = lax.optimization_barrier(jnp.sum(rounded.astype(jnp.float32), axis=0))
        return (hidden_grad, gate_terms, summed)
    hidden_all, gate_all, grad_all = lax.map(per_slot, slot_ids)
    expert_sums = jax.ops.segment_sum(grad_all, slot_expert, num_segments=slot_count)
    grad_total = expert_sums[slot_expert]
    new_first = beta_one * first_moment.astype(jnp.float32) + (1.0 - beta_one) * grad_total
    new_second = beta_two * second_moment.astype(jnp.float32) + (1.0 - beta_two) * grad_total * grad_total
    update = new_first / correct_one / (jnp.sqrt(new_second / correct_two) + epsilon) + decay_rate * master
    new_master = master - learn_rate * update
    hidden_grad = hidden_all.reshape(dev_count, slot_dev, dp_count, dev_count, capacity, hidden_count)
    hidden_grad = hidden_grad.transpose(2, 0, 3, 1, 4, 5)
    gate_grad = gate_all[target, dp_grid, dev_grid, position].reshape(dp_count * dev_count * tok_rows, top_count)
    return (hidden_grad, gate_grad, new_master, new_first.astype(jnp.bfloat16), new_second.astype(jnp.bfloat16))
```

```python
import jax
import jax.numpy as jnp
from jax import lax
from jax.experimental import pallas as pl
from jax.experimental.pallas import tpu as pltpu
from jax.sharding import PartitionSpec as P

HOT = 3
CORES = 2

beta_one = 0.9
beta_two = 0.95
learn_rate = 0.00022
decay_rate = 0.1
epsilon = 1e-08
correct_one = 0.6513215599
correct_two = 0.4012630607

bf16, f32 = jnp.bfloat16, jnp.float32


def matmul(spec, left, right):
    return jnp.einsum(spec, left, right, preferred_element_type=f32)


def dot(left, right, left_dim, right_dim, precision=None):
    return lax.dot_general(
        left,
        right,
        (((left_dim,), (right_dim,)), ((), ())),
        precision=precision,
        preferred_element_type=f32,
    )


def kernel_params():
    return pltpu.CompilerParams(vmem_limit_bytes=60 * 1024 * 1024)


def adam(grad, master, first, second):
    new_first = beta_one * first.astype(f32) + (1.0 - beta_one) * grad
    new_second = beta_two * second.astype(f32) + (1.0 - beta_two) * grad * grad
    update = (new_first * (1.0 / correct_one)) / (
        jnp.sqrt(new_second * (1.0 / correct_two)) + epsilon
    ) + decay_rate * master
    return master - learn_rate * update, new_first.astype(bf16), new_second.astype(bf16)


def gate(values, waits):
    def body(*refs):
        pass

    return pl.pallas_call(
        body,
        out_shape=[jax.ShapeDtypeStruct(v.shape, v.dtype) for v in values],
        in_specs=[pl.BlockSpec(memory_space=pl.ANY)] * (len(values) + len(waits)),
        out_specs=[pl.BlockSpec(memory_space=pl.ANY)] * len(values),
        input_output_aliases={i: i for i in range(len(values))},
        cost_estimate=light(),
    )(*values, *waits)


def column_hits(columns, gates, capacity):
    by_token = dot(columns, gates, 1, 1)
    live = by_token > 0
    tokens = gates.shape[0]
    row = lax.broadcasted_iota(jnp.int32, (tokens, tokens), 0)
    col = lax.broadcasted_iota(jnp.int32, (tokens, tokens), 1)
    earlier = jnp.where(row < col, 1.0, 0.0).astype(bf16)
    spot = dot(jnp.where(live, 1.0, 0.0).astype(bf16), earlier, 1, 0).astype(jnp.int32)
    spot = jnp.where(live, spot, -1)
    places = lax.broadcasted_iota(jnp.int32, (capacity, tokens), 0)

    def hit(at):
        return jnp.where(spot[at : at + 1] == places, 1.0, 0.0)

    return by_token, hit


def light():
    return pl.CostEstimate(flops=1, bytes_accessed=1, transcendentals=0)


def route_tables(columns, gates, slot_dev, capacity):
    peers, tokens, slots = gates[0].shape

    def body(columns_ref, ng_ref, fg_ref, hit_ref, back_ref, scale_ref):
        for at in range(4):
            plane, peer = at // 2, at % 2
            source_gates = (ng_ref, fg_ref)[plane][peer]
            by_token, hit = column_hits(columns_ref[...], source_gates, capacity)
            for l in range(slot_dev):
                hits = hit(l)
                hit_ref[plane, peer, l] = hits.astype(bf16)
                back_ref[plane, peer, l] = (hits * by_token[l : l + 1]).astype(bf16)
                at_expert = slot_dev + l
                scale = hit(at_expert) * by_token[at_expert : at_expert + 1]
                scale_ref[plane, peer, l] = scale.astype(bf16)

    gate_spec = pl.BlockSpec((2, tokens, slots), lambda q: (q, 0, 0))
    hit_spec = pl.BlockSpec((2, 2, slot_dev, capacity, tokens), lambda q: (0, q, 0, 0, 0))
    hit_shape = jax.ShapeDtypeStruct((2, peers, slot_dev, capacity, tokens), bf16)
    return pl.pallas_call(
        body,
        grid=(peers // 2,),
        out_shape=[hit_shape] * 3,
        in_specs=[pl.BlockSpec(columns.shape, lambda q: (0, 0)), gate_spec, gate_spec],
        out_specs=[hit_spec] * 3,
        compiler_params=kernel_params(),
        cost_estimate=light(),
    )(columns, *gates)


def add_planes(sums, wait):
    count, slot_dev, tokens = sums.shape

    def body(sums_ref, wait_ref, out_ref):
        out_ref[...] = sums_ref[: count // 2] + sums_ref[count // 2 :]

    return pl.pallas_call(
        body,
        in_specs=[
            pl.BlockSpec(memory_space=pltpu.VMEM),
            pl.BlockSpec(memory_space=pl.ANY),
        ],
        out_shape=jax.ShapeDtypeStruct((count // 2, slot_dev, tokens), f32),
        cost_estimate=light(),
    )(sums, wait)


def cast_weight(master, waits):
    slot_dev, shard_rows, features = master.shape
    block = (1, shard_rows, features)

    def body(*refs):
        refs[-1][...] = refs[0][...].astype(bf16)

    return pl.pallas_call(
        body,
        grid=(slot_dev,),
        in_specs=[pl.BlockSpec(block, lambda l: (l, 0, 0))]
        + [pl.BlockSpec(memory_space=pl.ANY)] * len(waits),
        out_specs=pl.BlockSpec(block, lambda l: (l, 0, 0)),
        out_shape=jax.ShapeDtypeStruct(master.shape, bf16),
        compiler_params=kernel_params(),
        cost_estimate=light(),
    )(master, *waits)


def split_hidden(plane, hidden):
    devs, slot_dev, capacity, width = hidden.shape
    block = (devs // 2, slot_dev, capacity, width // 2)

    def body(plane_ref, own_ref, other_ref, own_out, other_out):
        own_out[...] = own_ref[...]
        other_out[...] = other_ref[...]

    out_spec = pl.BlockSpec(block, lambda i, plane: (i, 0, 0, 0))
    shape = jax.ShapeDtypeStruct((devs, slot_dev, capacity, width // 2), bf16)
    return pl.pallas_call(
        body,
        grid_spec=pltpu.PrefetchScalarGridSpec(
            num_scalar_prefetch=1,
            grid=(2,),
            in_specs=[
                pl.BlockSpec(block, lambda i, plane: (i, 0, 0, plane[0])),
                pl.BlockSpec(block, lambda i, plane: (i, 0, 0, 1 - plane[0])),
            ],
            out_specs=[out_spec, out_spec],
        ),
        out_shape=[shape, shape],
        compiler_params=kernel_params(),
        cost_estimate=light(),
    )(plane, hidden, hidden)


def hot_part(columns, gates, rows, pairs):
    slots, capacity, width = rows.shape
    planes = 2

    def body(columns_ref, gates_ref, rows_ref, pairs_ref, out_ref):
        _, hit = column_hits(columns_ref[...], gates_ref[...], capacity)
        slots_of = jnp.concatenate([hit(s) for s in range(slots)], axis=0).astype(bf16)
        hots = jnp.concatenate([hit(slots + j) for j in range(HOT)], axis=0).astype(bf16)
        moved = (dot(hots, slots_of, 1, 1) * pairs_ref[...]).astype(bf16)
        table = dot(moved, rows_ref[...].reshape(slots * capacity, width), 1, 0).astype(bf16)
        for x in range(planes):
            part = table[:, x * (width // planes) : (x + 1) * (width // planes)]
            out_ref[x] = part.reshape(HOT, capacity, width // planes)

    return pl.pallas_call(
        body,
        out_shape=jax.ShapeDtypeStruct((planes, HOT, capacity, width // planes), bf16),
        compiler_params=kernel_params(),
        cost_estimate=light(),
    )(columns, gates, rows, pairs)


def whole_spec(shape):
    return pl.BlockSpec(shape, lambda *_: (0,) * len(shape))


def project_set(sources, peers, core, pieces, weights, hits, backs, rows, keep):
    devs, slot_dev, capacity, plane_rows = rows[0].shape
    tok_rows = hits.shape[-1]
    shard_rows, features = weights[0].shape[1:]
    total = len(sources) * tok_rows
    count = len(pieces)
    far_count = sum(plane for plane, _ in sources)
    counts = (len(sources) - far_count, far_count)

    def body(peers_ref, core_ref, *refs):
        token_refs = refs[:count]
        own_ref, other_ref, hit_ref, scatter_ref, nr_ref, fr_ref = refs[count : count + 6]
        near_ref, far_ref, sums_ref = refs[count + 6 : count + 9]
        weight_scr, group_ref = refs[-1 if keep else -2], refs[-2 if keep else -1]
        slot = pl.program_id(0)

        @pl.when(slot == 0)
        def _():
            start = 0
            for ref in token_refs:
                group_ref[start : start + ref.shape[0], :] = ref[...]
                start += ref.shape[0]

        sums = [0.0] * len(sources)
        scatters = [scatter_ref[p, peers_ref[k], slot].astype(f32) for p, k in sources]
        row_gates = [jnp.sum(scatter, axis=1, keepdims=True) for scatter in scatters]
        weight_scr[:shard_rows] = own_ref[0]
        weight_scr[shard_rows:] = other_ref[0]
        both = dot(group_ref[...], weight_scr[...], 1, 1).astype(bf16)
        for j in range(CORES):
            half = pl.multiple_of((core_ref[0] ^ j) * shard_rows, shard_rows)
            projected = both[:, j * shard_rows : (j + 1) * shard_rows]
            filled = [0, 0]
            for at, (plane, index) in enumerate(sources):
                peer = peers_ref[index]
                mine = projected[at * tok_rows : (at + 1) * tok_rows]
                picked = dot(hit_ref[plane, peer, slot], mine, 1, 0)
                saved = (nr_ref, fr_ref)[plane][peer, slot, :, pl.ds(half, shard_rows)]
                sums[at] = sums[at] + jnp.sum(saved.astype(f32) * picked, axis=1, keepdims=True)
                out_ref = (near_ref, far_ref)[plane]
                back = (row_gates[at] * picked).astype(bf16)
                out_ref[filled[plane], 0, :, pl.ds(half, shard_rows)] = back
                filled[plane] += 1
        for at, (plane, index) in enumerate(sources):
            hits = hit_ref[plane, peers_ref[index], slot].astype(f32)
            sums_ref[0, at : at + 1] = jnp.sum(hits * sums[at], axis=0, keepdims=True)

    def back_spec(number):
        return pl.BlockSpec((number, 1, capacity, plane_rows), lambda l, p, c: (0, l, 0, 0))

    def back_shape(number):
        return jax.ShapeDtypeStruct((number, slot_dev, capacity, plane_rows), bf16)

    weight_spec = pl.BlockSpec((1, shard_rows, features), lambda l, p, c: (l, 0, 0))
    return pl.pallas_call(
        body,
        grid_spec=pltpu.PrefetchScalarGridSpec(
            num_scalar_prefetch=2,
            grid=(slot_dev,),
            in_specs=[whole_spec(t.shape) for t in pieces]
            + [
                weight_spec,
                weight_spec,
                whole_spec(hits.shape),
                whole_spec(backs.shape),
                whole_spec(rows[0].shape),
                whole_spec(rows[1].shape),
            ],
            out_specs=[
                back_spec(counts[0]),
                back_spec(counts[1]),
                pl.BlockSpec((1, len(sources), tok_rows), lambda l, p, c: (l, 0, 0)),
            ]
            + ([whole_spec((total, features))] if keep else []),
            scratch_shapes=[pltpu.VMEM((CORES * shard_rows, features), bf16)]
            + ([] if keep else [pltpu.VMEM((total, features), bf16)]),
        ),
        out_shape=[
            back_shape(counts[0]),
            back_shape(counts[1]),
            jax.ShapeDtypeStruct((slot_dev, len(sources), tok_rows), f32),
        ]
        + ([jax.ShapeDtypeStruct((total, features), bf16)] if keep else []),
        compiler_params=kernel_params(),
        cost_estimate=pl.CostEstimate(
            flops=2 * total * features * slot_dev * plane_rows,
            bytes_accessed=2 * features * (2 * total + slot_dev * plane_rows),
            transcendentals=0,
        ),
    )(peers, core, *pieces, *weights, hits, backs, *rows)


def hidden_parts(peers, plane, near, far, near_order, far_order):
    slot_dev, capacity, plane_rows = near[0].shape[1:]
    devs = peers.shape[0]

    def body(peers_ref, plane_ref, *refs):
        out_ref = refs[-1]
        for arrays, order, flip in (
            (refs[: len(near)], near_order, 0),
            (refs[len(near) : -1], far_order, 1),
        ):
            half = pl.multiple_of((plane_ref[0] ^ flip) * plane_rows, plane_rows)
            flat = [ref.at[i] for ref in arrays for i in range(ref.shape[0])]
            for ref, index in zip(flat, order):
                out_ref[peers_ref[index], :, :, pl.ds(half, plane_rows)] = ref[...]

    shape = (devs, slot_dev, capacity, 2 * plane_rows)
    return pl.pallas_call(
        body,
        grid_spec=pltpu.PrefetchScalarGridSpec(
            num_scalar_prefetch=2,
            grid=(1,),
            in_specs=[whole_spec(v.shape) for v in (*near, *far)],
            out_specs=whole_spec(shape),
        ),
        out_shape=jax.ShapeDtypeStruct(shape, bf16),
        compiler_params=kernel_params(),
        cost_estimate=light(),
    )(peers, plane, *near, *far)


def scaled_rows(places, own_expert, scales, rows, table):
    slot_dev, capacity, plane_rows = rows[0].shape[1:]
    tok_rows = scales.shape[-1]
    width = slot_dev * plane_rows
    sources = places.shape[0]

    def body(places_ref, expert_ref, scale_ref, nr_ref, fr_ref, table_ref, out_ref):
        group = pl.program_id(0)
        for at in range(4):
            plane, peer = places_ref[4 * group + at, 0], places_ref[4 * group + at, 1]
            for l in range(slot_dev):
                expert = expert_ref[l]
                hot = table_ref[peer, plane, jnp.minimum(expert, HOT - 1)]
                own = jnp.where(plane == 0, nr_ref[peer, l], fr_ref[peer, l])
                picked = jnp.where(expert < HOT, hot, own)
                part = dot(picked, scale_ref[plane, peer, l], 0, 0).astype(bf16)
                out_ref[
                    l * plane_rows : (l + 1) * plane_rows, at * tok_rows : (at + 1) * tok_rows
                ] = part

    return pl.pallas_call(
        body,
        grid_spec=pltpu.PrefetchScalarGridSpec(
            num_scalar_prefetch=2,
            grid=(sources // 4,),
            in_specs=[
                whole_spec(scales.shape),
                whole_spec(rows[0].shape),
                whole_spec(rows[1].shape),
                whole_spec(table.shape),
            ],
            out_specs=pl.BlockSpec((width, 4 * tok_rows), lambda g, p, e: (0, g)),
        ),
        out_shape=jax.ShapeDtypeStruct((width, sources * tok_rows), bf16),
        compiler_params=kernel_params(),
        cost_estimate=light(),
    )(places, own_expert, scales, *rows, table)


def early_grad(groups, scaled):
    width, total = scaled.shape
    features = groups[0].shape[1]
    tile = 512 if features % 512 == 0 else features

    def body(*refs):
        scaled_ref, out_ref = refs[-2:]
        grad, start = 0.0, 0
        for ref in refs[:-2]:
            depth = ref.shape[0]
            grad = grad + dot(scaled_ref[:, start : start + depth], ref[...], 1, 0)
            start += depth
        out_ref[...] = grad.astype(bf16)

    return pl.pallas_call(
        body,
        grid=(features // tile,),
        in_specs=[pl.BlockSpec((g.shape[0], tile), lambda n: (0, n)) for g in groups]
        + [whole_spec(scaled.shape)],
        out_specs=pl.BlockSpec((width, tile), lambda n: (0, n)),
        out_shape=jax.ShapeDtypeStruct((width, features), bf16),
        compiler_params=kernel_params(),
        cost_estimate=pl.CostEstimate(
            flops=2 * total * features * width,
            bytes_accessed=2 * features * (total + width),
            transcendentals=0,
        ),
    )(*groups, scaled)


def last_grad(chunk, pieces, scaled, early, state=None):
    slot_dev, _, shard_rows, columns = scaled.shape
    total = sum(piece.shape[0] for piece in pieces)
    part = columns // total - 1
    features = pieces[0].shape[1]
    tile = 896 if state is None else 512
    tile = tile if features % tile == 0 else features
    count = len(pieces)

    def body(chunk_ref, *refs):
        scaled_ref, early_ref = refs[count : count + 2]
        last_ref = refs[-1]
        start = 0
        for ref in refs[:count]:
            last_ref[start : start + ref.shape[0], :] = ref[...]
            start += ref.shape[0]
        for l in range(slot_dev):
            grad = dot(scaled_ref[l, 0], last_ref[...], 1, 0) + early_ref[l, 0].astype(f32)
            if state is None:
                refs[count + 2][l] = grad.astype(bf16)
            else:
                given, master, first, second, o_master, o_first, o_second = refs[count + 2 : -1]
                grad = grad + given[l].astype(f32)
                o_master[l], o_first[l], o_second[l] = adam(grad, master[l], first[l], second[l])

    shard = pl.BlockSpec((slot_dev, shard_rows, tile), lambda n, chunk: (0, 0, n))
    shape = (slot_dev, shard_rows, features)
    outs = [bf16] if state is None else [f32, bf16, bf16]
    extra = () if state is None else state
    return pl.pallas_call(
        body,
        grid_spec=pltpu.PrefetchScalarGridSpec(
            num_scalar_prefetch=1,
            grid=(features // tile,),
            in_specs=[pl.BlockSpec((t.shape[0], tile), lambda n, chunk: (0, n)) for t in pieces]
            + [
                pl.BlockSpec(
                    (slot_dev, 1, shard_rows, total), lambda n, chunk: (0, chunk[0], 0, part)
                ),
                pl.BlockSpec(
                    (slot_dev, 1, shard_rows, tile), lambda n, chunk: (0, chunk[0], 0, n)
                ),
            ]
            + [shard] * len(extra),
            out_specs=[shard] * len(outs),
            scratch_shapes=[pltpu.VMEM((total, tile), bf16)],
        ),
        out_shape=[jax.ShapeDtypeStruct(shape, kind) for kind in outs],
        compiler_params=kernel_params(),
        cost_estimate=light()
        if state is None
        else pl.CostEstimate(
            flops=2 * total * features * slot_dev * shard_rows,
            bytes_accessed=2 * total * features + 24 * slot_dev * shard_rows * features,
            transcendentals=0,
        ),
    )(chunk, *pieces, scaled, early, *extra)


def on_device(
    grad_out,
    gate_probs,
    expert_route,
    replica_pick,
    slot_expert,
    saved_hidden,
    master,
    first_moment,
    second_moment,
):
    dp_count = lax.axis_size("dp")
    dev_count = lax.axis_size("expert")
    planes = dp_count // CORES
    slot_count = slot_expert.shape[0]
    slot_dev = slot_count // dev_count
    capacity, hidden_count = saved_hidden.shape[4:]
    tok_rows, top_count = gate_probs.shape
    feature_count = grad_out.shape[1]
    shard_rows = master.shape[1]
    plane_rows = CORES * shard_rows
    width = slot_dev * plane_rows
    dp_index = lax.axis_index("dp")
    dev_index = lax.axis_index("expert")
    plane, core = dp_index // CORES, dp_index % CORES

    def from_plane(value, shift):
        pairs = [(i, (i + shift * CORES) % dp_count) for i in range(dp_count)]
        return lax.ppermute(value, "dp", pairs)

    def from_sibling(value):
        return lax.ppermute(value, "dp", [(i, i ^ 1) for i in range(dp_count)])

    def from_peer(value, bits):
        return lax.ppermute(value, "expert", [(i, i ^ bits) for i in range(dev_count)])

    slot_ids = jnp.arange(slot_count, dtype=jnp.int32)
    same_expert = slot_expert[:, None] == slot_expert[None, :]
    slot_rank = jnp.sum(same_expert & (slot_ids[None, :] < slot_ids[:, None]), axis=1)
    host_mask = slot_expert[None, None, :] == expert_route[:, :, None]
    copy_count = jnp.sum(host_mask.astype(jnp.int32), axis=2)
    chosen = host_mask & (slot_rank == (replica_pick % copy_count)[:, :, None])
    slot_gates = jnp.sum(
        jnp.where(chosen, gate_probs.astype(bf16)[:, :, None], 0).astype(f32), axis=1
    ).astype(bf16)
    copies = jnp.broadcast_to(slot_gates[None], (dp_count * dev_count, tok_rows, slot_count))
    all_gates = lax.all_to_all(copies, ("dp", "expert"), split_axis=0, concat_axis=0, tiled=True)
    all_gates = all_gates.reshape(planes, CORES, dev_count, tok_rows, slot_count)
    all_gates = lax.dynamic_index_in_dim(all_gates, core, 1, keepdims=False)

    first_slot = dev_index * slot_dev
    own_ids = first_slot + jnp.arange(slot_dev, dtype=jnp.int32)
    own_expert = lax.dynamic_slice_in_dim(slot_expert, first_slot, slot_dev)
    hot_ids = jnp.arange(HOT, dtype=jnp.int32)
    columns = jnp.concatenate(
        [
            slot_ids[:, None] == own_ids[None, :],
            slot_expert[:, None] == own_expert[None, :],
            slot_expert[:, None] == hot_ids[None, :],
        ],
        axis=1,
    ).astype(bf16)
    hot_own = (own_expert[:, None] == hot_ids[None, :]).astype(bf16)

    def by_plane(values):
        if planes == 2:
            flip = plane == 1
            return [jnp.where(flip, values[1 - i], values[i]) for i in range(2)]
        stacked = jnp.stack(values)
        order = (plane - jnp.arange(planes)) % planes
        return list(jnp.take(stacked, order, axis=0))

    def finish(hidden_grad, gate_sums, state):
        by_slot = gate_sums.transpose(1, 0, 2).reshape(tok_rows, slot_count)
        gate_grad = jnp.sum(jnp.where(chosen, by_slot[:, None, :], 0.0), axis=2)
        return (hidden_grad[None, None], gate_grad, *state)

    if planes == 2 and dev_count == 8:
        columns = jnp.pad(columns, ((0, 0), (0, 16 - columns.shape[1]))).T
        gates = [
            lax.dynamic_index_in_dim(all_gates, (plane + i) % planes, 0, keepdims=False)
            for i in range(planes)
        ]
        ends = dev_index // 2
        inner = (ends == 1) | (ends == 2)

        def arrival(index):
            return jnp.where(inner & (index >= 4), index ^ 2, index)

        everyone = jnp.arange(dev_count, dtype=jnp.int32)
        peers = dev_index ^ arrival(everyone)
        position = arrival(dev_index ^ everyone)

        def along(value, moves):
            pairs = [(2 * i + y, 2 * j + y) for i, j in moves for y in range(2)]
            return lax.ppermute(value, "expert", pairs)

        across, outward = [(1, 2), (2, 1)], [(1, 0), (2, 3)]
        middle = tok_rows // 2

        pair = from_peer(grad_out, 2)
        mid = along(grad_out, across)
        side_0 = from_peer(grad_out, 1)
        far_0 = from_plane(grad_out, 1)
        plane_at = plane.astype(jnp.int32).reshape(1)
        near_rows, far_rows = split_hidden(plane_at, saved_hidden[0, 0])
        rows = (near_rows, from_plane(far_rows, 1))
        raw = lax.all_to_all(saved_hidden[0, 0], "expert", split_axis=0, concat_axis=0, tiled=True)
        raw = raw.reshape(slot_count, capacity, hidden_count)
        diag_0 = from_peer(far_0, 1)
        pair, mid, raw = gate((pair, mid, raw), (side_0, rows[1], diag_0, slot_gates))

        slot_hits, slot_backs, scales = route_tables(columns, gates, slot_dev, capacity)
        core_at = core.astype(jnp.int32).reshape(1)

        def project(sources, pieces, keep=True):
            return project_set(
                sources, peers, core_at, pieces, weights, slot_hits, slot_backs, rows, keep
            )

        every = jnp.concatenate([slot_ids, hot_ids])
        is_hot = jnp.arange(every.shape[0]) >= slot_count
        chooser = jnp.where(
            is_hot[:, None], slot_expert[None, :] == every[:, None], slot_ids == every[:, None]
        )
        chooser = jnp.pad(chooser.astype(bf16), ((0, -every.shape[0] % 16), (0, 0)))
        pairs = (hot_ids[:, None] == slot_expert[None, :]).astype(f32)
        pairs = jnp.repeat(jnp.repeat(pairs, capacity, axis=0), capacity, axis=1)

        moved_mid = along(mid, outward)
        moved_pair = along(pair, across)
        side_1, far_1 = from_peer(pair, 1), from_plane(pair, 1)
        table = hot_part(chooser, slot_gates, raw, pairs)
        table = [
            lax.dynamic_index_in_dim(table, (plane + i) % planes, 0, keepdims=False)
            for i in range(planes)
        ]
        table_far = from_plane(table[1], 1)

        mid, moved_mid, moved_pair, side_1, far_1, table_far = gate(
            (mid, moved_mid, moved_pair, side_1, far_1, table_far), (scales,)
        )
        own_weight = cast_weight(master, (moved_mid,))
        weights = (own_weight, from_sibling(own_weight))
        second = jnp.where(inner, mid, moved_mid)
        last = along(moved_pair, outward)
        side_2, far_2 = from_peer(second, 1), from_plane(second, 1)
        diag_1 = from_plane(side_1, 1)
        table = jnp.stack([table[0], table_far])
        table_side = from_peer(table, 1)
        order_a = ((0, 0), (0, 2), (1, 0), (0, 1), (0, 4), (0, 3), (1, 2))
        set_a = project(order_a, (grad_out, pair, far_0, side_0, second, side_1, far_1))
        (table_side,) = gate((table_side,), (last,))
        even = dev_index % 2 == 0
        table = jnp.stack([jnp.where(even, table, table_side), jnp.where(even, table_side, table)])
        lines = [list(range(y, dev_count, 2)) for y in range(2)]
        table = lax.all_gather(table[None], "expert", axis_index_groups=lines, tiled=True)
        table = table.reshape(dev_count, *table.shape[2:])

        moved_pair, last, side_2, far_2 = gate(
            (moved_pair, last, side_2, far_2), (diag_1, set_a[2])
        )
        third = jnp.where(inner, moved_pair, last)
        side_3, far_3 = from_peer(third, 1), from_plane(third, 1)
        order_b = ((1, 1), (1, 3), (1, 4), (0, 5), (0, 6))
        set_b = project(order_b, (diag_0, diag_1, far_2, side_2, third))
        top_2 = from_peer(far_2[:middle], 1)
        low_2 = from_plane(side_2[middle:], 1)

        side_3, far_3 = gate((side_3, far_3), (top_2, low_2, set_b[2]))
        top_3 = from_peer(far_3[:middle], 1)
        low_3 = from_plane(side_3[middle:], 1)
        order_d = ((1, 6), (0, 7), (1, 5), (1, 7))
        pieces = (far_3, side_3, top_2, low_2, top_3, low_3)

        sources = [*order_a, *order_b, *order_d]
        at_planes = jnp.array([p for p, _ in sources], jnp.int32)
        at_peers = peers[jnp.array([k for _, k in sources], jnp.int32)]
        (places,) = gate((jnp.stack([at_planes, at_peers], axis=1),), (set_b[2],))
        scaled = scaled_rows(places, own_expert, scales, rows, table)
        early = early_grad([set_a[3], set_b[3]], scaled)
        early = early.reshape(slot_dev, CORES, shard_rows, feature_count)
        scaled = scaled.reshape(slot_dev, CORES, shard_rows, -1)
        (given,) = last_grad(1 - core_at, pieces, scaled, early)
        given = from_sibling(given)
        set_d = project(order_d, pieces, keep=False)
        state = last_grad(
            core_at, pieces, scaled, early, (given, master, first_moment, second_moment)
        )

        sets = (set_a, set_b, set_d)
        far_backs = gate([from_plane(s[1], 1) for s in sets], (state[1],))
        hidden_grad = hidden_parts(
            peers,
            plane_at,
            [s[0] for s in sets],
            far_backs,
            [k for p, k in sources if p == 0],
            [k for p, k in sources if p == 1],
        )
        sums = jnp.concatenate([s[2] for s in sets], axis=1)
        ranks = [[sources.index((p, k)) for k in range(dev_count)] for p in range(planes)]
        sums = sums[:, jnp.array(ranks, jnp.int32)[:, position]].transpose(1, 2, 0, 3)
        sums = jnp.stack(by_plane([sums[0], sums[1]])).reshape(-1, slot_dev, tok_rows)
        cores = [
            [(x * CORES + c) * dev_count + d for x in range(planes) for d in range(dev_count)]
            for c in range(CORES)
        ]
        sums = lax.all_to_all(
            sums, ("dp", "expert"), 0, 0, axis_index_groups=cores, tiled=True
        )
        sums = add_planes(sums, state[1]).transpose(0, 2, 1)
        return finish(hidden_grad, sums, state)

    hidden = saved_hidden[0, 0].reshape(dev_count, slot_dev, capacity, planes, plane_rows)

    def hidden_for(shift):
        at = (plane + shift) % planes
        return lax.dynamic_index_in_dim(hidden, at, 3, keepdims=False)

    rows = [hidden_for(0)] + [from_plane(hidden_for(i), i) for i in range(1, planes)]

    own_weight = master.astype(bf16)
    other_weight = from_sibling(own_weight)
    weight = jnp.stack([own_weight, other_weight], axis=1)
    weight = jnp.where(core == 0, weight, weight[:, ::-1]).reshape(width, feature_count)
    before = (jnp.arange(tok_rows)[:, None] > jnp.arange(tok_rows)[None, :]).astype(bf16)
    places = jnp.arange(capacity, dtype=jnp.int32)
    gates = matmul("xqts,sk->xqkt", all_gates, columns)
    live = gates > 0
    spot = matmul("ut,xqkt->xqku", before, live.astype(bf16)).astype(jnp.int32)
    hits = (live[..., None, :] & (spot[..., None, :] == places[:, None])).astype(bf16)
    gates = gates[:, :, : 2 * slot_dev].astype(bf16)

    moved = matmul("xqjat,xqlct->xqjalc", hits[:, :, 2 * slot_dev :], hits[:, :, :slot_dev])
    moved = moved.astype(bf16) * hot_own.T[None, None, :, None, :, None]
    moved = [moved[i] for i in range(planes)]
    hot_rows = [
        matmul("qjalc,qlch->qjah", a, b).astype(bf16) for a, b in zip(moved, by_plane(rows))
    ]
    hot_rows = lax.psum(jnp.stack(hot_rows), "expert")

    def expert_rows(shift, own):
        table = lax.dynamic_index_in_dim(hot_rows, (plane - shift) % planes, 0, keepdims=False)
        picked = own
        for j in range(HOT):
            picked = jnp.where((own_expert == j)[None, :, None, None], table[:, j, None], picked)
        return picked

    def project(tokens, source_gates, source_hits, own):
        count = source_hits.shape[0]
        projected = matmul("td,hd->th", tokens, weight)
        projected = projected.reshape(count, tok_rows, slot_dev, plane_rows)
        slot_hits = source_hits[:, :slot_dev]
        spread = matmul("qlct,qlch->qtlh", slot_hits, own)
        gate_sums = jnp.sum(spread * projected, axis=3)
        scatter = slot_hits * source_gates[:, :slot_dev, None, :]
        back = matmul("qlct,qtlh->qlch", scatter, projected.astype(bf16)).astype(bf16)
        return gate_sums, back

    def scale(source_gates, source_hits, expert_own):
        count = source_hits.shape[0]
        scatter = source_hits[:, slot_dev : 2 * slot_dev] * source_gates[:, slot_dev:, None, :]
        scaled = matmul("qlct,qlch->qtlh", scatter, expert_own).astype(bf16)
        return scaled.reshape(count * tok_rows, width)

    def step(carry, at):
        tokens, total = carry
        shift, own = at
        gathered = lax.all_gather(tokens, "expert", tiled=True)
        source = (plane - shift) % planes
        source_gates = lax.dynamic_index_in_dim(gates, source, 0, keepdims=False)
        source_hits = lax.dynamic_index_in_dim(hits, source, 0, keepdims=False)
        sums, back = project(gathered, source_gates, source_hits, own)
        scaled = scale(source_gates, source_hits, expert_rows(shift, own))
        total = total + matmul("th,td->hd", scaled, gathered)
        return (from_plane(tokens, 1), total), (sums, back)

    start = (grad_out, jnp.zeros((width, feature_count), f32))
    (_, grads), (sums, backs) = lax.scan(step, start, (jnp.arange(planes), jnp.stack(rows)))

    backs = [backs[0]] + [from_plane(backs[i], -i) for i in range(1, planes)]
    order = (jnp.arange(planes) - plane) % planes
    hidden_grad = jnp.concatenate(list(jnp.take(jnp.stack(backs), order, axis=0)), axis=-1)
    gate_sums = sums[0]
    for i in range(1, planes):
        gate_sums = gate_sums + from_plane(sums[i], -i)

    grads = grads.reshape(slot_dev, CORES, shard_rows, feature_count)
    kept = lax.dynamic_index_in_dim(grads, core, 1, keepdims=False)
    given = lax.dynamic_index_in_dim(grads, 1 - core, 1, keepdims=False)
    grad_total = kept + from_sibling(given.astype(bf16)).astype(f32)
    state = adam(grad_total, master, first_moment, second_moment)
    gate_sums = lax.all_to_all(gate_sums, "expert", split_axis=0, concat_axis=0, tiled=True)
    return finish(hidden_grad, gate_sums, state)


def solution(mesh):
    placed = (
        P(("dp", "expert"), None),
        P(("dp", "expert"), None),
        P(("dp", "expert"), None),
        P(("dp", "expert"), None),
        P(),
        P("dp", "expert", None, None, None, None),
        P("expert", "dp", None),
        P("expert", "dp", None),
        P("expert", "dp", None),
    )
    return jax.shard_map(
        on_device,
        mesh=mesh,
        in_specs=placed,
        out_specs=(
            P("dp", "expert", None, None, None, None),
            P(("dp", "expert"), None),
            P("expert", "dp", None),
            P("expert", "dp", None),
            P("expert", "dp", None),
        ),
        check_vma=False,
    )
```

```python
import jax
import jax.numpy as jnp
from jax import lax
from jax.experimental import pallas as pl
from jax.experimental.pallas import tpu as pltpu
from jax.sharding import PartitionSpec as P

HOT = 3
CORES = 2

beta_one = 0.9
beta_two = 0.95
learn_rate = 0.00022
decay_rate = 0.1
epsilon = 1e-08
correct_one = 0.6513215599
correct_two = 0.4012630607

bf16, f32 = jnp.bfloat16, jnp.float32


def matmul(spec, left, right):
    return jnp.einsum(spec, left, right, preferred_element_type=f32)


def dot(left, right, left_dim, right_dim, precision=None):
    return lax.dot_general(
        left,
        right,
        (((left_dim,), (right_dim,)), ((), ())),
        precision=precision,
        preferred_element_type=f32,
    )


def kernel_params():
    return pltpu.CompilerParams(vmem_limit_bytes=60 * 1024 * 1024)


def adam(grad, master, first, second):
    new_first = beta_one * first.astype(f32) + (1.0 - beta_one) * grad
    new_second = beta_two * second.astype(f32) + (1.0 - beta_two) * grad * grad
    update = (new_first * (1.0 / correct_one)) / (
        jnp.sqrt(new_second * (1.0 / correct_two)) + epsilon
    ) + decay_rate * master
    return master - learn_rate * update, new_first.astype(bf16), new_second.astype(bf16)


def gate(values, waits):
    def body(*refs):
        pass

    return pl.pallas_call(
        body,
        out_shape=[jax.ShapeDtypeStruct(v.shape, v.dtype) for v in values],
        in_specs=[pl.BlockSpec(memory_space=pl.ANY)] * (len(values) + len(waits)),
        out_specs=[pl.BlockSpec(memory_space=pl.ANY)] * len(values),
        input_output_aliases={i: i for i in range(len(values))},
        cost_estimate=light(),
    )(*values, *waits)


def column_hits(columns, gates, capacity):
    by_token = dot(columns, gates, 1, 1)
    live = by_token > 0
    tokens = gates.shape[0]
    row = lax.broadcasted_iota(jnp.int32, (tokens, tokens), 0)
    col = lax.broadcasted_iota(jnp.int32, (tokens, tokens), 1)
    earlier = jnp.where(row < col, 1.0, 0.0).astype(bf16)
    spot = dot(jnp.where(live, 1.0, 0.0).astype(bf16), earlier, 1, 0).astype(jnp.int32)
    spot = jnp.where(live, spot, -1)
    places = lax.broadcasted_iota(jnp.int32, (capacity, tokens), 0)

    def hit(at):
        return jnp.where(spot[at : at + 1] == places, 1.0, 0.0)

    return by_token, hit


def light():
    return pl.CostEstimate(flops=1, bytes_accessed=1, transcendentals=0)


def route_tables(columns, gates, slot_dev, capacity):
    peers, tokens, slots = gates[0].shape

    def body(columns_ref, ng_ref, fg_ref, hit_ref, back_ref, scale_ref):
        for at in range(4):
            plane, peer = at // 2, at % 2
            source_gates = (ng_ref, fg_ref)[plane][peer]
            by_token, hit = column_hits(columns_ref[...], source_gates, capacity)
            for l in range(slot_dev):
                hits = hit(l)
                hit_ref[plane, peer, l] = hits.astype(bf16)
                back_ref[plane, peer, l] = (hits * by_token[l : l + 1]).astype(bf16)
                at_expert = slot_dev + l
                scale = hit(at_expert) * by_token[at_expert : at_expert + 1]
                scale_ref[plane, peer, l] = scale.astype(bf16)

    gate_spec = pl.BlockSpec((2, tokens, slots), lambda q: (q, 0, 0))
    hit_spec = pl.BlockSpec((2, 2, slot_dev, capacity, tokens), lambda q: (0, q, 0, 0, 0))
    hit_shape = jax.ShapeDtypeStruct((2, peers, slot_dev, capacity, tokens), bf16)
    return pl.pallas_call(
        body,
        grid=(peers // 2,),
        out_shape=[hit_shape] * 3,
        in_specs=[pl.BlockSpec(columns.shape, lambda q: (0, 0)), gate_spec, gate_spec],
        out_specs=[hit_spec] * 3,
        compiler_params=kernel_params(),
        cost_estimate=light(),
    )(columns, *gates)


def add_planes(sums, wait):
    count, slot_dev, tokens = sums.shape

    def body(sums_ref, wait_ref, out_ref):
        out_ref[...] = sums_ref[: count // 2] + sums_ref[count // 2 :]

    return pl.pallas_call(
        body,
        in_specs=[
            pl.BlockSpec(memory_space=pltpu.VMEM),
            pl.BlockSpec(memory_space=pl.ANY),
        ],
        out_shape=jax.ShapeDtypeStruct((count // 2, slot_dev, tokens), f32),
        cost_estimate=light(),
    )(sums, wait)


def cast_weight(master, waits):
    slot_dev, shard_rows, features = master.shape
    block = (1, shard_rows, features)

    def body(*refs):
        refs[-1][...] = refs[0][...].astype(bf16)

    return pl.pallas_call(
        body,
        grid=(slot_dev,),
        in_specs=[pl.BlockSpec(block, lambda l: (l, 0, 0))]
        + [pl.BlockSpec(memory_space=pl.ANY)] * len(waits),
        out_specs=pl.BlockSpec(block, lambda l: (l, 0, 0)),
        out_shape=jax.ShapeDtypeStruct(master.shape, bf16),
        compiler_params=kernel_params(),
        cost_estimate=light(),
    )(master, *waits)


def split_hidden(plane, hidden):
    devs, slot_dev, capacity, width = hidden.shape
    block = (devs // 2, slot_dev, capacity, width // 2)

    def body(plane_ref, own_ref, other_ref, own_out, other_out):
        own_out[...] = own_ref[...]
        other_out[...] = other_ref[...]

    out_spec = pl.BlockSpec(block, lambda i, plane: (i, 0, 0, 0))
    shape = jax.ShapeDtypeStruct((devs, slot_dev, capacity, width // 2), bf16)
    return pl.pallas_call(
        body,
        grid_spec=pltpu.PrefetchScalarGridSpec(
            num_scalar_prefetch=1,
            grid=(2,),
            in_specs=[
                pl.BlockSpec(block, lambda i, plane: (i, 0, 0, plane[0])),
                pl.BlockSpec(block, lambda i, plane: (i, 0, 0, 1 - plane[0])),
            ],
            out_specs=[out_spec, out_spec],
        ),
        out_shape=[shape, shape],
        compiler_params=kernel_params(),
        cost_estimate=light(),
    )(plane, hidden, hidden)


def hot_part(columns, gates, rows, pairs):
    slots, capacity, width = rows.shape
    planes = 2

    def body(columns_ref, gates_ref, rows_ref, pairs_ref, out_ref):
        _, hit = column_hits(columns_ref[...], gates_ref[...], capacity)
        slots_of = jnp.concatenate([hit(s) for s in range(slots)], axis=0).astype(bf16)
        hots = jnp.concatenate([hit(slots + j) for j in range(HOT)], axis=0).astype(bf16)
        moved = (dot(hots, slots_of, 1, 1) * pairs_ref[...]).astype(bf16)
        table = dot(moved, rows_ref[...].reshape(slots * capacity, width), 1, 0).astype(bf16)
        for x in range(planes):
            part = table[:, x * (width // planes) : (x + 1) * (width // planes)]
            out_ref[x] = part.reshape(HOT, capacity, width // planes)

    return pl.pallas_call(
        body,
        out_shape=jax.ShapeDtypeStruct((planes, HOT, capacity, width // planes), bf16),
        compiler_params=kernel_params(),
        cost_estimate=light(),
    )(columns, gates, rows, pairs)


def whole_spec(shape):
    return pl.BlockSpec(shape, lambda *_: (0,) * len(shape))


def project_set(sources, peers, core, pieces, weights, hits, backs, rows, keep):
    devs, slot_dev, capacity, plane_rows = rows[0].shape
    tok_rows = hits.shape[-1]
    shard_rows, features = weights[0].shape[1:]
    total = len(sources) * tok_rows
    count = len(pieces)
    far_count = sum(plane for plane, _ in sources)
    counts = (len(sources) - far_count, far_count)

    def body(peers_ref, core_ref, *refs):
        token_refs = refs[:count]
        own_ref, other_ref, hit_ref, scatter_ref, nr_ref, fr_ref = refs[count : count + 6]
        near_ref, far_ref, sums_ref = refs[count + 6 : count + 9]
        weight_scr, group_ref = refs[-1 if keep else -2], refs[-2 if keep else -1]
        slot = pl.program_id(0)

        @pl.when(slot == 0)
        def _():
            start = 0
            for ref in token_refs:
                group_ref[start : start + ref.shape[0], :] = ref[...]
                start += ref.shape[0]

        sums = [0.0] * len(sources)
        scatters = [scatter_ref[p, peers_ref[k], slot].astype(f32) for p, k in sources]
        row_gates = [jnp.sum(scatter, axis=1, keepdims=True) for scatter in scatters]
        weight_scr[:shard_rows] = own_ref[0]
        weight_scr[shard_rows:] = other_ref[0]
        both = dot(group_ref[...], weight_scr[...], 1, 1).astype(bf16)
        for j in range(CORES):
            half = pl.multiple_of((core_ref[0] ^ j) * shard_rows, shard_rows)
            projected = both[:, j * shard_rows : (j + 1) * shard_rows]
            filled = [0, 0]
            for at, (plane, index) in enumerate(sources):
                peer = peers_ref[index]
                mine = projected[at * tok_rows : (at + 1) * tok_rows]
                picked = dot(hit_ref[plane, peer, slot], mine, 1, 0)
                saved = (nr_ref, fr_ref)[plane][peer, slot, :, pl.ds(half, shard_rows)]
                sums[at] = sums[at] + jnp.sum(saved.astype(f32) * picked, axis=1, keepdims=True)
                out_ref = (near_ref, far_ref)[plane]
                back = (row_gates[at] * picked).astype(bf16)
                out_ref[filled[plane], 0, :, pl.ds(half, shard_rows)] = back
                filled[plane] += 1
        for at, (plane, index) in enumerate(sources):
            hits = hit_ref[plane, peers_ref[index], slot].astype(f32)
            sums_ref[0, at : at + 1] = jnp.sum(hits * sums[at], axis=0, keepdims=True)

    def back_spec(number):
        return pl.BlockSpec((number, 1, capacity, plane_rows), lambda l, p, c: (0, l, 0, 0))

    def back_shape(number):
        return jax.ShapeDtypeStruct((number, slot_dev, capacity, plane_rows), bf16)

    weight_spec = pl.BlockSpec((1, shard_rows, features), lambda l, p, c: (l, 0, 0))
    return pl.pallas_call(
        body,
        grid_spec=pltpu.PrefetchScalarGridSpec(
            num_scalar_prefetch=2,
            grid=(slot_dev,),
            in_specs=[whole_spec(t.shape) for t in pieces]
            + [
                weight_spec,
                weight_spec,
                whole_spec(hits.shape),
                whole_spec(backs.shape),
                whole_spec(rows[0].shape),
                whole_spec(rows[1].shape),
            ],
            out_specs=[
                back_spec(counts[0]),
                back_spec(counts[1]),
                pl.BlockSpec((1, len(sources), tok_rows), lambda l, p, c: (l, 0, 0)),
            ]
            + ([whole_spec((total, features))] if keep else []),
            scratch_shapes=[pltpu.VMEM((CORES * shard_rows, features), bf16)]
            + ([] if keep else [pltpu.VMEM((total, features), bf16)]),
        ),
        out_shape=[
            back_shape(counts[0]),
            back_shape(counts[1]),
            jax.ShapeDtypeStruct((slot_dev, len(sources), tok_rows), f32),
        ]
        + ([jax.ShapeDtypeStruct((total, features), bf16)] if keep else []),
        compiler_params=kernel_params(),
        cost_estimate=pl.CostEstimate(
            flops=2 * total * features * slot_dev * plane_rows,
            bytes_accessed=2 * features * (2 * total + slot_dev * plane_rows),
            transcendentals=0,
        ),
    )(peers, core, *pieces, *weights, hits, backs, *rows)


def hidden_parts(peers, plane, near, far, near_order, far_order):
    slot_dev, capacity, plane_rows = near[0].shape[1:]
    devs = peers.shape[0]

    def body(peers_ref, plane_ref, *refs):
        out_ref = refs[-1]
        for arrays, order, flip in (
            (refs[: len(near)], near_order, 0),
            (refs[len(near) : -1], far_order, 1),
        ):
            half = pl.multiple_of((plane_ref[0] ^ flip) * plane_rows, plane_rows)
            flat = [ref.at[i] for ref in arrays for i in range(ref.shape[0])]
            for ref, index in zip(flat, order):
                out_ref[peers_ref[index], :, :, pl.ds(half, plane_rows)] = ref[...]

    shape = (devs, slot_dev, capacity, 2 * plane_rows)
    return pl.pallas_call(
        body,
        grid_spec=pltpu.PrefetchScalarGridSpec(
            num_scalar_prefetch=2,
            grid=(1,),
            in_specs=[whole_spec(v.shape) for v in (*near, *far)],
            out_specs=whole_spec(shape),
        ),
        out_shape=jax.ShapeDtypeStruct(shape, bf16),
        compiler_params=kernel_params(),
        cost_estimate=light(),
    )(peers, plane, *near, *far)


def scaled_rows(places, own_expert, scales, rows, table):
    slot_dev, capacity, plane_rows = rows[0].shape[1:]
    tok_rows = scales.shape[-1]
    width = slot_dev * plane_rows
    sources = places.shape[0]

    def body(places_ref, expert_ref, scale_ref, nr_ref, fr_ref, table_ref, out_ref):
        group = pl.program_id(0)
        for at in range(4):
            plane, peer = places_ref[4 * group + at, 0], places_ref[4 * group + at, 1]
            for l in range(slot_dev):
                expert = expert_ref[l]
                hot = table_ref[peer, plane, jnp.minimum(expert, HOT - 1)]
                own = jnp.where(plane == 0, nr_ref[peer, l], fr_ref[peer, l])
                picked = jnp.where(expert < HOT, hot, own)
                part = dot(picked, scale_ref[plane, peer, l], 0, 0).astype(bf16)
                out_ref[
                    l * plane_rows : (l + 1) * plane_rows, at * tok_rows : (at + 1) * tok_rows
                ] = part

    return pl.pallas_call(
        body,
        grid_spec=pltpu.PrefetchScalarGridSpec(
            num_scalar_prefetch=2,
            grid=(sources // 4,),
            in_specs=[
                whole_spec(scales.shape),
                whole_spec(rows[0].shape),
                whole_spec(rows[1].shape),
                whole_spec(table.shape),
            ],
            out_specs=pl.BlockSpec((width, 4 * tok_rows), lambda g, p, e: (0, g)),
        ),
        out_shape=jax.ShapeDtypeStruct((width, sources * tok_rows), bf16),
        compiler_params=kernel_params(),
        cost_estimate=light(),
    )(places, own_expert, scales, *rows, table)


def early_grad(groups, scaled):
    width, total = scaled.shape
    features = groups[0].shape[1]
    tile = 512 if features % 512 == 0 else features

    def body(*refs):
        scaled_ref, out_ref = refs[-2:]
        grad, start = 0.0, 0
        for ref in refs[:-2]:
            depth = ref.shape[0]
            grad = grad + dot(scaled_ref[:, start : start + depth], ref[...], 1, 0)
            start += depth
        out_ref[...] = grad.astype(bf16)

    return pl.pallas_call(
        body,
        grid=(features // tile,),
        in_specs=[pl.BlockSpec((g.shape[0], tile), lambda n: (0, n)) for g in groups]
        + [whole_spec(scaled.shape)],
        out_specs=pl.BlockSpec((width, tile), lambda n: (0, n)),
        out_shape=jax.ShapeDtypeStruct((width, features), bf16),
        compiler_params=kernel_params(),
        cost_estimate=pl.CostEstimate(
            flops=2 * total * features * width,
            bytes_accessed=2 * features * (total + width),
            transcendentals=0,
        ),
    )(*groups, scaled)


def last_grad(chunk, pieces, scaled, early, state=None):
    slot_dev, _, shard_rows, columns = scaled.shape
    total = sum(piece.shape[0] for piece in pieces)
    part = columns // total - 1
    features = pieces[0].shape[1]
    tile = 896 if state is None else 512
    tile = tile if features % tile == 0 else features
    count = len(pieces)

    def body(chunk_ref, *refs):
        scaled_ref, early_ref = refs[count : count + 2]
        last_ref = refs[-1]
        start = 0
        for ref in refs[:count]:
            last_ref[start : start + ref.shape[0], :] = ref[...]
            start += ref.shape[0]
        for l in range(slot_dev):
            grad = dot(scaled_ref[l, 0], last_ref[...], 1, 0) + early_ref[l, 0].astype(f32)
            if state is None:
                refs[count + 2][l] = grad.astype(bf16)
            else:
                given, master, first, second, o_master, o_first, o_second = refs[count + 2 : -1]
                grad = grad + given[l].astype(f32)
                o_master[l], o_first[l], o_second[l] = adam(grad, master[l], first[l], second[l])

    shard = pl.BlockSpec((slot_dev, shard_rows, tile), lambda n, chunk: (0, 0, n))
    shape = (slot_dev, shard_rows, features)
    outs = [bf16] if state is None else [f32, bf16, bf16]
    extra = () if state is None else state
    return pl.pallas_call(
        body,
        grid_spec=pltpu.PrefetchScalarGridSpec(
            num_scalar_prefetch=1,
            grid=(features // tile,),
            in_specs=[pl.BlockSpec((t.shape[0], tile), lambda n, chunk: (0, n)) for t in pieces]
            + [
                pl.BlockSpec(
                    (slot_dev, 1, shard_rows, total), lambda n, chunk: (0, chunk[0], 0, part)
                ),
                pl.BlockSpec(
                    (slot_dev, 1, shard_rows, tile), lambda n, chunk: (0, chunk[0], 0, n)
                ),
            ]
            + [shard] * len(extra),
            out_specs=[shard] * len(outs),
            scratch_shapes=[pltpu.VMEM((total, tile), bf16)],
        ),
        out_shape=[jax.ShapeDtypeStruct(shape, kind) for kind in outs],
        compiler_params=kernel_params(),
        cost_estimate=light()
        if state is None
        else pl.CostEstimate(
            flops=2 * total * features * slot_dev * shard_rows,
            bytes_accessed=2 * total * features + 24 * slot_dev * shard_rows * features,
            transcendentals=0,
        ),
    )(chunk, *pieces, scaled, early, *extra)


def on_device(
    grad_out,
    gate_probs,
    expert_route,
    replica_pick,
    slot_expert,
    saved_hidden,
    master,
    first_moment,
    second_moment,
):
    dp_count = lax.axis_size("dp")
    dev_count = lax.axis_size("expert")
    planes = dp_count // CORES
    slot_count = slot_expert.shape[0]
    slot_dev = slot_count // dev_count
    capacity, hidden_count = saved_hidden.shape[4:]
    tok_rows, top_count = gate_probs.shape
    feature_count = grad_out.shape[1]
    shard_rows = master.shape[1]
    plane_rows = CORES * shard_rows
    width = slot_dev * plane_rows
    dp_index = lax.axis_index("dp")
    dev_index = lax.axis_index("expert")
    plane, core = dp_index // CORES, dp_index % CORES

    def from_plane(value, shift):
        pairs = [(i, (i + shift * CORES) % dp_count) for i in range(dp_count)]
        return lax.ppermute(value, "dp", pairs)

    def from_sibling(value):
        return lax.ppermute(value, "dp", [(i, i ^ 1) for i in range(dp_count)])

    def from_peer(value, bits):
        return lax.ppermute(value, "expert", [(i, i ^ bits) for i in range(dev_count)])

    slot_ids = jnp.arange(slot_count, dtype=jnp.int32)
    same_expert = slot_expert[:, None] == slot_expert[None, :]
    slot_rank = jnp.sum(same_expert & (slot_ids[None, :] < slot_ids[:, None]), axis=1)
    host_mask = slot_expert[None, None, :] == expert_route[:, :, None]
    copy_count = jnp.sum(host_mask.astype(jnp.int32), axis=2)
    chosen = host_mask & (slot_rank == (replica_pick % copy_count)[:, :, None])
    slot_gates = jnp.sum(
        jnp.where(chosen, gate_probs.astype(bf16)[:, :, None], 0).astype(f32), axis=1
    ).astype(bf16)
    copies = jnp.broadcast_to(slot_gates[None], (dp_count * dev_count, tok_rows, slot_count))
    all_gates = lax.all_to_all(copies, ("dp", "expert"), split_axis=0, concat_axis=0, tiled=True)
    all_gates = all_gates.reshape(planes, CORES, dev_count, tok_rows, slot_count)
    all_gates = lax.dynamic_index_in_dim(all_gates, core, 1, keepdims=False)

    first_slot = dev_index * slot_dev
    own_ids = first_slot + jnp.arange(slot_dev, dtype=jnp.int32)
    own_expert = lax.dynamic_slice_in_dim(slot_expert, first_slot, slot_dev)
    hot_ids = jnp.arange(HOT, dtype=jnp.int32)
    columns = jnp.concatenate(
        [
            slot_ids[:, None] == own_ids[None, :],
            slot_expert[:, None] == own_expert[None, :],
            slot_expert[:, None] == hot_ids[None, :],
        ],
        axis=1,
    ).astype(bf16)
    hot_own = (own_expert[:, None] == hot_ids[None, :]).astype(bf16)

    def by_plane(values):
        if planes == 2:
            flip = plane == 1
            return [jnp.where(flip, values[1 - i], values[i]) for i in range(2)]
        stacked = jnp.stack(values)
        order = (plane - jnp.arange(planes)) % planes
        return list(jnp.take(stacked, order, axis=0))

    def finish(hidden_grad, gate_sums, state):
        by_slot = gate_sums.transpose(1, 0, 2).reshape(tok_rows, slot_count)
        gate_grad = jnp.sum(jnp.where(chosen, by_slot[:, None, :], 0.0), axis=2)
        return (hidden_grad[None, None], gate_grad, *state)

    if planes == 2 and dev_count == 8:
        columns = jnp.pad(columns, ((0, 0), (0, 16 - columns.shape[1]))).T
        gates = [
            lax.dynamic_index_in_dim(all_gates, (plane + i) % planes, 0, keepdims=False)
            for i in range(planes)
        ]
        ends = dev_index // 2
        inner = (ends == 1) | (ends == 2)

        def arrival(index):
            return jnp.where(inner & (index >= 4), index ^ 2, index)

        everyone = jnp.arange(dev_count, dtype=jnp.int32)
        peers = dev_index ^ arrival(everyone)
        position = arrival(dev_index ^ everyone)

        def along(value, moves):
            pairs = [(2 * i + y, 2 * j + y) for i, j in moves for y in range(2)]
            return lax.ppermute(value, "expert", pairs)

        across, outward = [(1, 2), (2, 1)], [(1, 0), (2, 3)]
        middle = tok_rows // 2

        pair = from_peer(grad_out, 2)
        mid = along(grad_out, across)
        side_0 = from_peer(grad_out, 1)
        far_0 = from_plane(grad_out, 1)
        plane_at = plane.astype(jnp.int32).reshape(1)
        near_rows, far_rows = split_hidden(plane_at, saved_hidden[0, 0])
        rows = (near_rows, from_plane(far_rows, 1))
        raw = lax.all_to_all(saved_hidden[0, 0], "expert", split_axis=0, concat_axis=0, tiled=True)
        raw = raw.reshape(slot_count, capacity, hidden_count)
        diag_0 = from_peer(far_0, 1)
        pair, mid, raw = gate((pair, mid, raw), (side_0, rows[1], diag_0, slot_gates))

        slot_hits, slot_backs, scales = route_tables(columns, gates, slot_dev, capacity)
        core_at = core.astype(jnp.int32).reshape(1)

        def project(sources, pieces, keep=True):
            return project_set(
                sources, peers, core_at, pieces, weights, slot_hits, slot_backs, rows, keep
            )

        every = jnp.concatenate([slot_ids, hot_ids])
        is_hot = jnp.arange(every.shape[0]) >= slot_count
        chooser = jnp.where(
            is_hot[:, None], slot_expert[None, :] == every[:, None], slot_ids == every[:, None]
        )
        chooser = jnp.pad(chooser.astype(bf16), ((0, -every.shape[0] % 16), (0, 0)))
        pairs = (hot_ids[:, None] == slot_expert[None, :]).astype(f32)
        pairs = jnp.repeat(jnp.repeat(pairs, capacity, axis=0), capacity, axis=1)

        moved_mid = along(mid, outward)
        moved_pair = along(pair, across)
        side_1, far_1 = from_peer(pair, 1), from_plane(pair, 1)
        table = hot_part(chooser, slot_gates, raw, pairs)
        table = [
            lax.dynamic_index_in_dim(table, (plane + i) % planes, 0, keepdims=False)
            for i in range(planes)
        ]
        table_far = from_plane(table[1], 1)

        mid, moved_mid, moved_pair, side_1, far_1, table_far = gate(
            (mid, moved_mid, moved_pair, side_1, far_1, table_far), (scales,)
        )
        own_weight = cast_weight(master, (moved_mid,))
        weights = (own_weight, from_sibling(own_weight))
        second = jnp.where(inner, mid, moved_mid)
        last = along(moved_pair, outward)
        side_2, far_2 = from_peer(second, 1), from_plane(second, 1)
        diag_1 = from_plane(side_1, 1)
        table = jnp.stack([table[0], table_far])
        table_side = from_peer(table, 1)
        order_a = ((0, 0), (0, 2), (1, 0), (0, 1), (0, 4), (0, 3), (1, 2))
        set_a = project(order_a, (grad_out, pair, far_0, side_0, second, side_1, far_1))
        (table_side,) = gate((table_side,), (last, side_2, far_2))
        even = dev_index % 2 == 0
        table = jnp.stack([jnp.where(even, table, table_side), jnp.where(even, table_side, table)])
        lines = [list(range(y, dev_count, 2)) for y in range(2)]
        table = lax.all_gather(table[None], "expert", axis_index_groups=lines, tiled=True)
        table = table.reshape(dev_count, *table.shape[2:])

        moved_pair, last, side_2, far_2 = gate(
            (moved_pair, last, side_2, far_2), (diag_1, set_a[2])
        )
        third = jnp.where(inner, moved_pair, last)
        side_3, far_3 = from_peer(third, 1), from_plane(third, 1)
        order_b = ((1, 1), (1, 3), (1, 4), (0, 5), (0, 6))
        set_b = project(order_b, (diag_0, diag_1, far_2, side_2, third))
        top_2 = from_peer(far_2[:middle], 1)
        low_2 = from_plane(side_2[middle:], 1)

        side_3, far_3 = gate((side_3, far_3), (top_2, low_2, set_b[2]))
        top_3 = from_peer(far_3[:middle], 1)
        low_3 = from_plane(side_3[middle:], 1)
        order_d = ((1, 6), (0, 7), (1, 5), (1, 7))
        pieces = (far_3, side_3, top_2, low_2, top_3, low_3)

        sources = [*order_a, *order_b, *order_d]
        at_planes = jnp.array([p for p, _ in sources], jnp.int32)
        at_peers = peers[jnp.array([k for _, k in sources], jnp.int32)]
        (places,) = gate((jnp.stack([at_planes, at_peers], axis=1),), (set_b[2],))
        scaled = scaled_rows(places, own_expert, scales, rows, table)
        early = early_grad([set_a[3], set_b[3]], scaled)
        early = early.reshape(slot_dev, CORES, shard_rows, feature_count)
        scaled = scaled.reshape(slot_dev, CORES, shard_rows, -1)
        (given,) = last_grad(1 - core_at, pieces, scaled, early)
        given = from_sibling(given)
        set_d = project(order_d, pieces, keep=False)
        state = last_grad(
            core_at, pieces, scaled, early, (given, master, first_moment, second_moment)
        )

        sets = (set_a, set_b, set_d)
        far_backs = gate([from_plane(s[1], 1) for s in sets], (state[1],))
        hidden_grad = hidden_parts(
            peers,
            plane_at,
            [s[0] for s in sets],
            far_backs,
            [k for p, k in sources if p == 0],
            [k for p, k in sources if p == 1],
        )
        sums = jnp.concatenate([s[2] for s in sets], axis=1)
        ranks = [[sources.index((p, k)) for k in range(dev_count)] for p in range(planes)]
        sums = sums[:, jnp.array(ranks, jnp.int32)[:, position]].transpose(1, 2, 0, 3)
        sums = jnp.stack(by_plane([sums[0], sums[1]])).reshape(-1, slot_dev, tok_rows)
        cores = [
            [(x * CORES + c) * dev_count + d for x in range(planes) for d in range(dev_count)]
            for c in range(CORES)
        ]
        sums = lax.all_to_all(
            sums, ("dp", "expert"), 0, 0, axis_index_groups=cores, tiled=True
        )
        sums = add_planes(sums, state[1]).transpose(0, 2, 1)
        return finish(hidden_grad, sums, state)

    hidden = saved_hidden[0, 0].reshape(dev_count, slot_dev, capacity, planes, plane_rows)

    def hidden_for(shift):
        at = (plane + shift) % planes
        return lax.dynamic_index_in_dim(hidden, at, 3, keepdims=False)

    rows = [hidden_for(0)] + [from_plane(hidden_for(i), i) for i in range(1, planes)]

    own_weight = master.astype(bf16)
    other_weight = from_sibling(own_weight)
    weight = jnp.stack([own_weight, other_weight], axis=1)
    weight = jnp.where(core == 0, weight, weight[:, ::-1]).reshape(width, feature_count)
    before = (jnp.arange(tok_rows)[:, None] > jnp.arange(tok_rows)[None, :]).astype(bf16)
    places = jnp.arange(capacity, dtype=jnp.int32)
    gates = matmul("xqts,sk->xqkt", all_gates, columns)
    live = gates > 0
    spot = matmul("ut,xqkt->xqku", before, live.astype(bf16)).astype(jnp.int32)
    hits = (live[..., None, :] & (spot[..., None, :] == places[:, None])).astype(bf16)
    gates = gates[:, :, : 2 * slot_dev].astype(bf16)

    moved = matmul("xqjat,xqlct->xqjalc", hits[:, :, 2 * slot_dev :], hits[:, :, :slot_dev])
    moved = moved.astype(bf16) * hot_own.T[None, None, :, None, :, None]
    moved = [moved[i] for i in range(planes)]
    hot_rows = [
        matmul("qjalc,qlch->qjah", a, b).astype(bf16) for a, b in zip(moved, by_plane(rows))
    ]
    hot_rows = lax.psum(jnp.stack(hot_rows), "expert")

    def expert_rows(shift, own):
        table = lax.dynamic_index_in_dim(hot_rows, (plane - shift) % planes, 0, keepdims=False)
        picked = own
        for j in range(HOT):
            picked = jnp.where((own_expert == j)[None, :, None, None], table[:, j, None], picked)
        return picked

    def project(tokens, source_gates, source_hits, own):
        count = source_hits.shape[0]
        projected = matmul("td,hd->th", tokens, weight)
        projected = projected.reshape(count, tok_rows, slot_dev, plane_rows)
        slot_hits = source_hits[:, :slot_dev]
        spread = matmul("qlct,qlch->qtlh", slot_hits, own)
        gate_sums = jnp.sum(spread * projected, axis=3)
        scatter = slot_hits * source_gates[:, :slot_dev, None, :]
        back = matmul("qlct,qtlh->qlch", scatter, projected.astype(bf16)).astype(bf16)
        return gate_sums, back

    def scale(source_gates, source_hits, expert_own):
        count = source_hits.shape[0]
        scatter = source_hits[:, slot_dev : 2 * slot_dev] * source_gates[:, slot_dev:, None, :]
        scaled = matmul("qlct,qlch->qtlh", scatter, expert_own).astype(bf16)
        return scaled.reshape(count * tok_rows, width)

    def step(carry, at):
        tokens, total = carry
        shift, own = at
        gathered = lax.all_gather(tokens, "expert", tiled=True)
        source = (plane - shift) % planes
        source_gates = lax.dynamic_index_in_dim(gates, source, 0, keepdims=False)
        source_hits = lax.dynamic_index_in_dim(hits, source, 0, keepdims=False)
        sums, back = project(gathered, source_gates, source_hits, own)
        scaled = scale(source_gates, source_hits, expert_rows(shift, own))
        total = total + matmul("th,td->hd", scaled, gathered)
        return (from_plane(tokens, 1), total), (sums, back)

    start = (grad_out, jnp.zeros((width, feature_count), f32))
    (_, grads), (sums, backs) = lax.scan(step, start, (jnp.arange(planes), jnp.stack(rows)))

    backs = [backs[0]] + [from_plane(backs[i], -i) for i in range(1, planes)]
    order = (jnp.arange(planes) - plane) % planes
    hidden_grad = jnp.concatenate(list(jnp.take(jnp.stack(backs), order, axis=0)), axis=-1)
    gate_sums = sums[0]
    for i in range(1, planes):
        gate_sums = gate_sums + from_plane(sums[i], -i)

    grads = grads.reshape(slot_dev, CORES, shard_rows, feature_count)
    kept = lax.dynamic_index_in_dim(grads, core, 1, keepdims=False)
    given = lax.dynamic_index_in_dim(grads, 1 - core, 1, keepdims=False)
    grad_total = kept + from_sibling(given.astype(bf16)).astype(f32)
    state = adam(grad_total, master, first_moment, second_moment)
    gate_sums = lax.all_to_all(gate_sums, "expert", split_axis=0, concat_axis=0, tiled=True)
    return finish(hidden_grad, gate_sums, state)


def solution(mesh):
    placed = (
        P(("dp", "expert"), None),
        P(("dp", "expert"), None),
        P(("dp", "expert"), None),
        P(("dp", "expert"), None),
        P(),
        P("dp", "expert", None, None, None, None),
        P("expert", "dp", None),
        P("expert", "dp", None),
        P("expert", "dp", None),
    )
    return jax.shard_map(
        on_device,
        mesh=mesh,
        in_specs=placed,
        out_specs=(
            P("dp", "expert", None, None, None, None),
            P(("dp", "expert"), None),
            P("expert", "dp", None),
            P("expert", "dp", None),
            P("expert", "dp", None),
        ),
        check_vma=False,
    )
```

```python
import jax
import jax.numpy as jnp
from jax import lax
from jax.experimental import pallas as pl
from jax.experimental.pallas import tpu as pltpu
from jax.sharding import PartitionSpec as P

HOT = 3
CORES = 2

beta_one = 0.9
beta_two = 0.95
learn_rate = 0.00022
decay_rate = 0.1
epsilon = 1e-08
correct_one = 0.6513215599
correct_two = 0.4012630607

bf16, f32 = jnp.bfloat16, jnp.float32


def matmul(spec, left, right):
    return jnp.einsum(spec, left, right, preferred_element_type=f32)


def dot(left, right, left_dim, right_dim, precision=None):
    return lax.dot_general(
        left,
        right,
        (((left_dim,), (right_dim,)), ((), ())),
        precision=precision,
        preferred_element_type=f32,
    )


def kernel_params():
    return pltpu.CompilerParams(vmem_limit_bytes=60 * 1024 * 1024)


def adam(grad, master, first, second):
    new_first = beta_one * first.astype(f32) + (1.0 - beta_one) * grad
    new_second = beta_two * second.astype(f32) + (1.0 - beta_two) * grad * grad
    update = (new_first * (1.0 / correct_one)) / (
        jnp.sqrt(new_second * (1.0 / correct_two)) + epsilon
    ) + decay_rate * master
    return master - learn_rate * update, new_first.astype(bf16), new_second.astype(bf16)


def gate(values, waits):
    def body(*refs):
        pass

    return pl.pallas_call(
        body,
        out_shape=[jax.ShapeDtypeStruct(v.shape, v.dtype) for v in values],
        in_specs=[pl.BlockSpec(memory_space=pl.ANY)] * (len(values) + len(waits)),
        out_specs=[pl.BlockSpec(memory_space=pl.ANY)] * len(values),
        input_output_aliases={i: i for i in range(len(values))},
        cost_estimate=light(),
    )(*values, *waits)


def column_hits(columns, gates, capacity):
    by_token = dot(columns, gates, 1, 1)
    live = by_token > 0
    tokens = gates.shape[0]
    row = lax.broadcasted_iota(jnp.int32, (tokens, tokens), 0)
    col = lax.broadcasted_iota(jnp.int32, (tokens, tokens), 1)
    earlier = jnp.where(row < col, 1.0, 0.0).astype(bf16)
    spot = dot(jnp.where(live, 1.0, 0.0).astype(bf16), earlier, 1, 0).astype(jnp.int32)
    spot = jnp.where(live, spot, -1)
    places = lax.broadcasted_iota(jnp.int32, (capacity, tokens), 0)

    def hit(at):
        return jnp.where(spot[at : at + 1] == places, 1.0, 0.0)

    return by_token, hit


def light():
    return pl.CostEstimate(flops=1, bytes_accessed=1, transcendentals=0)


def route_tables(columns, gates, slot_dev, capacity):
    peers, tokens, slots = gates[0].shape

    def body(columns_ref, ng_ref, fg_ref, hit_ref, back_ref, scale_ref):
        for at in range(4):
            plane, peer = at // 2, at % 2
            source_gates = (ng_ref, fg_ref)[plane][peer]
            by_token, hit = column_hits(columns_ref[...], source_gates, capacity)
            for l in range(slot_dev):
                hits = hit(l)
                hit_ref[plane, peer, l] = hits.astype(bf16)
                back_ref[plane, peer, l] = (hits * by_token[l : l + 1]).astype(bf16)
                at_expert = slot_dev + l
                scale = hit(at_expert) * by_token[at_expert : at_expert + 1]
                scale_ref[plane, peer, l] = scale.astype(bf16)

    gate_spec = pl.BlockSpec((2, tokens, slots), lambda q: (q, 0, 0))
    hit_spec = pl.BlockSpec((2, 2, slot_dev, capacity, tokens), lambda q: (0, q, 0, 0, 0))
    hit_shape = jax.ShapeDtypeStruct((2, peers, slot_dev, capacity, tokens), bf16)
    return pl.pallas_call(
        body,
        grid=(peers // 2,),
        out_shape=[hit_shape] * 3,
        in_specs=[pl.BlockSpec(columns.shape, lambda q: (0, 0)), gate_spec, gate_spec],
        out_specs=[hit_spec] * 3,
        compiler_params=kernel_params(),
        cost_estimate=light(),
    )(columns, *gates)


def add_planes(sums, wait):
    count, slot_dev, tokens = sums.shape

    def body(sums_ref, wait_ref, out_ref):
        out_ref[...] = sums_ref[: count // 2] + sums_ref[count // 2 :]

    return pl.pallas_call(
        body,
        in_specs=[
            pl.BlockSpec(memory_space=pltpu.VMEM),
            pl.BlockSpec(memory_space=pl.ANY),
        ],
        out_shape=jax.ShapeDtypeStruct((count // 2, slot_dev, tokens), f32),
        cost_estimate=light(),
    )(sums, wait)


def cast_weight(master, waits):
    slot_dev, shard_rows, features = master.shape
    block = (1, shard_rows, features)

    def body(*refs):
        refs[-1][...] = refs[0][...].astype(bf16)

    return pl.pallas_call(
        body,
        grid=(slot_dev,),
        in_specs=[pl.BlockSpec(block, lambda l: (l, 0, 0))]
        + [pl.BlockSpec(memory_space=pl.ANY)] * len(waits),
        out_specs=pl.BlockSpec(block, lambda l: (l, 0, 0)),
        out_shape=jax.ShapeDtypeStruct(master.shape, bf16),
        compiler_params=kernel_params(),
        cost_estimate=light(),
    )(master, *waits)


def split_hidden(plane, hidden):
    devs, slot_dev, capacity, width = hidden.shape
    block = (devs // 2, slot_dev, capacity, width // 2)

    def body(plane_ref, own_ref, other_ref, own_out, other_out):
        own_out[...] = own_ref[...]
        other_out[...] = other_ref[...]

    out_spec = pl.BlockSpec(block, lambda i, plane: (i, 0, 0, 0))
    shape = jax.ShapeDtypeStruct((devs, slot_dev, capacity, width // 2), bf16)
    return pl.pallas_call(
        body,
        grid_spec=pltpu.PrefetchScalarGridSpec(
            num_scalar_prefetch=1,
            grid=(2,),
            in_specs=[
                pl.BlockSpec(block, lambda i, plane: (i, 0, 0, plane[0])),
                pl.BlockSpec(block, lambda i, plane: (i, 0, 0, 1 - plane[0])),
            ],
            out_specs=[out_spec, out_spec],
        ),
        out_shape=[shape, shape],
        compiler_params=kernel_params(),
        cost_estimate=light(),
    )(plane, hidden, hidden)


def hot_part(columns, gates, rows, pairs):
    slots, capacity, width = rows.shape
    planes = 2

    def body(columns_ref, gates_ref, rows_ref, pairs_ref, out_ref):
        _, hit = column_hits(columns_ref[...], gates_ref[...], capacity)
        slots_of = jnp.concatenate([hit(s) for s in range(slots)], axis=0).astype(bf16)
        hots = jnp.concatenate([hit(slots + j) for j in range(HOT)], axis=0).astype(bf16)
        moved = (dot(hots, slots_of, 1, 1) * pairs_ref[...]).astype(bf16)
        table = dot(moved, rows_ref[...].reshape(slots * capacity, width), 1, 0).astype(bf16)
        for x in range(planes):
            part = table[:, x * (width // planes) : (x + 1) * (width // planes)]
            out_ref[x] = part.reshape(HOT, capacity, width // planes)

    return pl.pallas_call(
        body,
        out_shape=jax.ShapeDtypeStruct((planes, HOT, capacity, width // planes), bf16),
        compiler_params=kernel_params(),
        cost_estimate=light(),
    )(columns, gates, rows, pairs)


def whole_spec(shape):
    return pl.BlockSpec(shape, lambda *_: (0,) * len(shape))


def project_set(sources, peers, core, pieces, weights, hits, backs, rows, keep):
    devs, slot_dev, capacity, plane_rows = rows[0].shape
    tok_rows = hits.shape[-1]
    shard_rows, features = weights[0].shape[1:]
    total = len(sources) * tok_rows
    count = len(pieces)
    far_count = sum(plane for plane, _ in sources)
    counts = (len(sources) - far_count, far_count)

    def body(peers_ref, core_ref, *refs):
        token_refs = refs[:count]
        own_ref, other_ref, hit_ref, scatter_ref, nr_ref, fr_ref = refs[count : count + 6]
        near_ref, far_ref, sums_ref = refs[count + 6 : count + 9]
        weight_scr, group_ref = refs[-1 if keep else -2], refs[-2 if keep else -1]
        slot = pl.program_id(0)

        @pl.when(slot == 0)
        def _():
            start = 0
            for ref in token_refs:
                group_ref[start : start + ref.shape[0], :] = ref[...]
                start += ref.shape[0]

        sums = [0.0] * len(sources)
        scatters = [scatter_ref[p, peers_ref[k], slot].astype(f32) for p, k in sources]
        row_gates = [jnp.sum(scatter, axis=1, keepdims=True) for scatter in scatters]
        weight_scr[:shard_rows] = own_ref[0]
        weight_scr[shard_rows:] = other_ref[0]
        both = dot(group_ref[...], weight_scr[...], 1, 1).astype(bf16)
        for j in range(CORES):
            half = pl.multiple_of((core_ref[0] ^ j) * shard_rows, shard_rows)
            projected = both[:, j * shard_rows : (j + 1) * shard_rows]
            filled = [0, 0]
            for at, (plane, index) in enumerate(sources):
                peer = peers_ref[index]
                mine = projected[at * tok_rows : (at + 1) * tok_rows]
                picked = dot(hit_ref[plane, peer, slot], mine, 1, 0)
                saved = (nr_ref, fr_ref)[plane][peer, slot, :, pl.ds(half, shard_rows)]
                sums[at] = sums[at] + jnp.sum(saved.astype(f32) * picked, axis=1, keepdims=True)
                out_ref = (near_ref, far_ref)[plane]
                back = (row_gates[at] * picked).astype(bf16)
                out_ref[filled[plane], 0, :, pl.ds(half, shard_rows)] = back
                filled[plane] += 1
        for at, (plane, index) in enumerate(sources):
            hits = hit_ref[plane, peers_ref[index], slot].astype(f32)
            sums_ref[0, at : at + 1] = jnp.sum(hits * sums[at], axis=0, keepdims=True)

    def back_spec(number):
        return pl.BlockSpec((number, 1, capacity, plane_rows), lambda l, p, c: (0, l, 0, 0))

    def back_shape(number):
        return jax.ShapeDtypeStruct((number, slot_dev, capacity, plane_rows), bf16)

    weight_spec = pl.BlockSpec((1, shard_rows, features), lambda l, p, c: (l, 0, 0))
    return pl.pallas_call(
        body,
        grid_spec=pltpu.PrefetchScalarGridSpec(
            num_scalar_prefetch=2,
            grid=(slot_dev,),
            in_specs=[whole_spec(t.shape) for t in pieces]
            + [
                weight_spec,
                weight_spec,
                whole_spec(hits.shape),
                whole_spec(backs.shape),
                whole_spec(rows[0].shape),
                whole_spec(rows[1].shape),
            ],
            out_specs=[
                back_spec(counts[0]),
                back_spec(counts[1]),
                pl.BlockSpec((1, len(sources), tok_rows), lambda l, p, c: (l, 0, 0)),
            ]
            + ([whole_spec((total, features))] if keep else []),
            scratch_shapes=[pltpu.VMEM((CORES * shard_rows, features), bf16)]
            + ([] if keep else [pltpu.VMEM((total, features), bf16)]),
        ),
        out_shape=[
            back_shape(counts[0]),
            back_shape(counts[1]),
            jax.ShapeDtypeStruct((slot_dev, len(sources), tok_rows), f32),
        ]
        + ([jax.ShapeDtypeStruct((total, features), bf16)] if keep else []),
        compiler_params=kernel_params(),
        cost_estimate=pl.CostEstimate(
            flops=2 * total * features * slot_dev * plane_rows,
            bytes_accessed=2 * features * (2 * total + slot_dev * plane_rows),
            transcendentals=0,
        ),
    )(peers, core, *pieces, *weights, hits, backs, *rows)


def hidden_parts(peers, plane, near, far, wait, near_order, far_order):
    slot_dev, capacity, plane_rows = near[0].shape[1:]
    devs = peers.shape[0]

    def body(peers_ref, plane_ref, *refs):
        out_ref = refs[-1]
        for arrays, order, flip in (
            (refs[: len(near)], near_order, 0),
            (refs[len(near) : -2], far_order, 1),
        ):
            half = pl.multiple_of((plane_ref[0] ^ flip) * plane_rows, plane_rows)
            flat = [ref.at[i] for ref in arrays for i in range(ref.shape[0])]
            for ref, index in zip(flat, order):
                out_ref[peers_ref[index], :, :, pl.ds(half, plane_rows)] = ref[...]

    shape = (devs, slot_dev, capacity, 2 * plane_rows)
    return pl.pallas_call(
        body,
        grid_spec=pltpu.PrefetchScalarGridSpec(
            num_scalar_prefetch=2,
            grid=(1,),
            in_specs=[whole_spec(v.shape) for v in (*near, *far)]
            + [pl.BlockSpec(memory_space=pl.ANY)],
            out_specs=whole_spec(shape),
        ),
        out_shape=jax.ShapeDtypeStruct(shape, bf16),
        compiler_params=kernel_params(),
        cost_estimate=light(),
    )(peers, plane, *near, *far, wait)


def scaled_rows(places, own_expert, scales, rows, table):
    slot_dev, capacity, plane_rows = rows[0].shape[1:]
    tok_rows = scales.shape[-1]
    width = slot_dev * plane_rows
    sources = places.shape[0]

    def body(places_ref, expert_ref, scale_ref, nr_ref, fr_ref, table_ref, out_ref):
        group = pl.program_id(0)
        for at in range(4):
            plane, peer = places_ref[4 * group + at, 0], places_ref[4 * group + at, 1]
            for l in range(slot_dev):
                expert = expert_ref[l]
                hot = table_ref[peer, plane, jnp.minimum(expert, HOT - 1)]
                own = jnp.where(plane == 0, nr_ref[peer, l], fr_ref[peer, l])
                picked = jnp.where(expert < HOT, hot, own)
                part = dot(picked, scale_ref[plane, peer, l], 0, 0).astype(bf16)
                out_ref[
                    l * plane_rows : (l + 1) * plane_rows, at * tok_rows : (at + 1) * tok_rows
                ] = part

    return pl.pallas_call(
        body,
        grid_spec=pltpu.PrefetchScalarGridSpec(
            num_scalar_prefetch=2,
            grid=(sources // 4,),
            in_specs=[
                whole_spec(scales.shape),
                whole_spec(rows[0].shape),
                whole_spec(rows[1].shape),
                whole_spec(table.shape),
            ],
            out_specs=pl.BlockSpec((width, 4 * tok_rows), lambda g, p, e: (0, g)),
        ),
        out_shape=jax.ShapeDtypeStruct((width, sources * tok_rows), bf16),
        compiler_params=kernel_params(),
        cost_estimate=light(),
    )(places, own_expert, scales, *rows, table)


def early_grad(groups, scaled):
    width, total = scaled.shape
    features = groups[0].shape[1]
    tile = 512 if features % 512 == 0 else features

    def body(*refs):
        scaled_ref, out_ref = refs[-2:]
        grad, start = 0.0, 0
        for ref in refs[:-2]:
            depth = ref.shape[0]
            grad = grad + dot(scaled_ref[:, start : start + depth], ref[...], 1, 0)
            start += depth
        out_ref[...] = grad.astype(bf16)

    return pl.pallas_call(
        body,
        grid=(features // tile,),
        in_specs=[pl.BlockSpec((g.shape[0], tile), lambda n: (0, n)) for g in groups]
        + [whole_spec(scaled.shape)],
        out_specs=pl.BlockSpec((width, tile), lambda n: (0, n)),
        out_shape=jax.ShapeDtypeStruct((width, features), bf16),
        compiler_params=kernel_params(),
        cost_estimate=pl.CostEstimate(
            flops=2 * total * features * width,
            bytes_accessed=2 * features * (total + width),
            transcendentals=0,
        ),
    )(*groups, scaled)


def last_grad(chunk, pieces, scaled, early, state=None):
    slot_dev, _, shard_rows, columns = scaled.shape
    total = sum(piece.shape[0] for piece in pieces)
    part = columns // total - 1
    features = pieces[0].shape[1]
    tile = 896 if state is None else 512
    tile = tile if features % tile == 0 else features
    count = len(pieces)

    def body(chunk_ref, *refs):
        scaled_ref, early_ref = refs[count : count + 2]
        last_ref = refs[-1]
        start = 0
        for ref in refs[:count]:
            last_ref[start : start + ref.shape[0], :] = ref[...]
            start += ref.shape[0]
        for l in range(slot_dev):
            grad = dot(scaled_ref[l, 0], last_ref[...], 1, 0) + early_ref[l, 0].astype(f32)
            if state is None:
                refs[count + 2][l] = grad.astype(bf16)
            else:
                given, master, first, second, o_master, o_first, o_second = refs[count + 2 : -1]
                grad = grad + given[l].astype(f32)
                o_master[l], o_first[l], o_second[l] = adam(grad, master[l], first[l], second[l])

    shard = pl.BlockSpec((slot_dev, shard_rows, tile), lambda n, chunk: (0, 0, n))
    shape = (slot_dev, shard_rows, features)
    outs = [bf16] if state is None else [f32, bf16, bf16]
    extra = () if state is None else state
    return pl.pallas_call(
        body,
        grid_spec=pltpu.PrefetchScalarGridSpec(
            num_scalar_prefetch=1,
            grid=(features // tile,),
            in_specs=[pl.BlockSpec((t.shape[0], tile), lambda n, chunk: (0, n)) for t in pieces]
            + [
                pl.BlockSpec(
                    (slot_dev, 1, shard_rows, total), lambda n, chunk: (0, chunk[0], 0, part)
                ),
                pl.BlockSpec(
                    (slot_dev, 1, shard_rows, tile), lambda n, chunk: (0, chunk[0], 0, n)
                ),
            ]
            + [shard] * len(extra),
            out_specs=[shard] * len(outs),
            scratch_shapes=[pltpu.VMEM((total, tile), bf16)],
        ),
        out_shape=[jax.ShapeDtypeStruct(shape, kind) for kind in outs],
        compiler_params=kernel_params(),
        cost_estimate=light()
        if state is None
        else pl.CostEstimate(
            flops=2 * total * features * slot_dev * shard_rows,
            bytes_accessed=2 * total * features + 24 * slot_dev * shard_rows * features,
            transcendentals=0,
        ),
    )(chunk, *pieces, scaled, early, *extra)


def on_device(
    grad_out,
    gate_probs,
    expert_route,
    replica_pick,
    slot_expert,
    saved_hidden,
    master,
    first_moment,
    second_moment,
):
    dp_count = lax.axis_size("dp")
    dev_count = lax.axis_size("expert")
    planes = dp_count // CORES
    slot_count = slot_expert.shape[0]
    slot_dev = slot_count // dev_count
    capacity, hidden_count = saved_hidden.shape[4:]
    tok_rows, top_count = gate_probs.shape
    feature_count = grad_out.shape[1]
    shard_rows = master.shape[1]
    plane_rows = CORES * shard_rows
    width = slot_dev * plane_rows
    dp_index = lax.axis_index("dp")
    dev_index = lax.axis_index("expert")
    plane, core = dp_index // CORES, dp_index % CORES

    def from_plane(value, shift):
        pairs = [(i, (i + shift * CORES) % dp_count) for i in range(dp_count)]
        return lax.ppermute(value, "dp", pairs)

    def from_sibling(value):
        return lax.ppermute(value, "dp", [(i, i ^ 1) for i in range(dp_count)])

    def from_peer(value, bits):
        return lax.ppermute(value, "expert", [(i, i ^ bits) for i in range(dev_count)])

    slot_ids = jnp.arange(slot_count, dtype=jnp.int32)
    same_expert = slot_expert[:, None] == slot_expert[None, :]
    slot_rank = jnp.sum(same_expert & (slot_ids[None, :] < slot_ids[:, None]), axis=1)
    host_mask = slot_expert[None, None, :] == expert_route[:, :, None]
    copy_count = jnp.sum(host_mask.astype(jnp.int32), axis=2)
    chosen = host_mask & (slot_rank == (replica_pick % copy_count)[:, :, None])
    slot_gates = jnp.sum(
        jnp.where(chosen, gate_probs.astype(bf16)[:, :, None], 0).astype(f32), axis=1
    ).astype(bf16)
    copies = jnp.broadcast_to(slot_gates[None], (dp_count * dev_count, tok_rows, slot_count))
    all_gates = lax.all_to_all(copies, ("dp", "expert"), split_axis=0, concat_axis=0, tiled=True)
    all_gates = all_gates.reshape(planes, CORES, dev_count, tok_rows, slot_count)
    all_gates = lax.dynamic_index_in_dim(all_gates, core, 1, keepdims=False)

    first_slot = dev_index * slot_dev
    own_ids = first_slot + jnp.arange(slot_dev, dtype=jnp.int32)
    own_expert = lax.dynamic_slice_in_dim(slot_expert, first_slot, slot_dev)
    hot_ids = jnp.arange(HOT, dtype=jnp.int32)
    columns = jnp.concatenate(
        [
            slot_ids[:, None] == own_ids[None, :],
            slot_expert[:, None] == own_expert[None, :],
            slot_expert[:, None] == hot_ids[None, :],
        ],
        axis=1,
    ).astype(bf16)
    hot_own = (own_expert[:, None] == hot_ids[None, :]).astype(bf16)

    def by_plane(values):
        if planes == 2:
            flip = plane == 1
            return [jnp.where(flip, values[1 - i], values[i]) for i in range(2)]
        stacked = jnp.stack(values)
        order = (plane - jnp.arange(planes)) % planes
        return list(jnp.take(stacked, order, axis=0))

    def finish(hidden_grad, gate_sums, state):
        by_slot = gate_sums.transpose(1, 0, 2).reshape(tok_rows, slot_count)
        gate_grad = jnp.sum(jnp.where(chosen, by_slot[:, None, :], 0.0), axis=2)
        return (hidden_grad[None, None], gate_grad, *state)

    if planes == 2 and dev_count == 8:
        columns = jnp.pad(columns, ((0, 0), (0, 16 - columns.shape[1]))).T
        gates = [
            lax.dynamic_index_in_dim(all_gates, (plane + i) % planes, 0, keepdims=False)
            for i in range(planes)
        ]
        ends = dev_index // 2
        inner = (ends == 1) | (ends == 2)

        def arrival(index):
            return jnp.where(inner & (index >= 4), index ^ 2, index)

        everyone = jnp.arange(dev_count, dtype=jnp.int32)
        peers = dev_index ^ arrival(everyone)
        position = arrival(dev_index ^ everyone)

        def along(value, moves):
            pairs = [(2 * i + y, 2 * j + y) for i, j in moves for y in range(2)]
            return lax.ppermute(value, "expert", pairs)

        across, outward = [(1, 2), (2, 1)], [(1, 0), (2, 3)]
        middle = tok_rows // 2

        pair = from_peer(grad_out, 2)
        mid = along(grad_out, across)
        side_0 = from_peer(grad_out, 1)
        far_0 = from_plane(grad_out, 1)
        plane_at = plane.astype(jnp.int32).reshape(1)
        near_rows, far_rows = split_hidden(plane_at, saved_hidden[0, 0])
        rows = (near_rows, from_plane(far_rows, 1))
        raw = lax.all_to_all(saved_hidden[0, 0], "expert", split_axis=0, concat_axis=0, tiled=True)
        raw = raw.reshape(slot_count, capacity, hidden_count)
        diag_0 = from_peer(far_0, 1)
        pair, mid, raw = gate((pair, mid, raw), (side_0, rows[1], diag_0, slot_gates))

        slot_hits, slot_backs, scales = route_tables(columns, gates, slot_dev, capacity)
        core_at = core.astype(jnp.int32).reshape(1)

        def project(sources, pieces, keep=True):
            return project_set(
                sources, peers, core_at, pieces, weights, slot_hits, slot_backs, rows, keep
            )

        every = jnp.concatenate([slot_ids, hot_ids])
        is_hot = jnp.arange(every.shape[0]) >= slot_count
        chooser = jnp.where(
            is_hot[:, None], slot_expert[None, :] == every[:, None], slot_ids == every[:, None]
        )
        chooser = jnp.pad(chooser.astype(bf16), ((0, -every.shape[0] % 16), (0, 0)))
        pairs = (hot_ids[:, None] == slot_expert[None, :]).astype(f32)
        pairs = jnp.repeat(jnp.repeat(pairs, capacity, axis=0), capacity, axis=1)

        moved_mid = along(mid, outward)
        moved_pair = along(pair, across)
        side_1, far_1 = from_peer(pair, 1), from_plane(pair, 1)
        table = hot_part(chooser, slot_gates, raw, pairs)
        table = [
            lax.dynamic_index_in_dim(table, (plane + i) % planes, 0, keepdims=False)
            for i in range(planes)
        ]
        table_far = from_plane(table[1], 1)

        mid, moved_mid, moved_pair, side_1, far_1, table_far = gate(
            (mid, moved_mid, moved_pair, side_1, far_1, table_far), (scales,)
        )
        own_weight = cast_weight(master, (moved_mid,))
        weights = (own_weight, from_sibling(own_weight))
        second = jnp.where(inner, mid, moved_mid)
        last = along(moved_pair, outward)
        side_2, far_2 = from_peer(second, 1), from_plane(second, 1)
        diag_1 = from_plane(side_1, 1)
        (table,) = gate((jnp.stack([table[0], table_far]),), (last, side_2, far_2))
        table_side = from_peer(table, 1)
        order_a = ((0, 0), (0, 2), (1, 0), (0, 1), (0, 4), (0, 3), (1, 2))
        set_a = project(order_a, (grad_out, pair, far_0, side_0, second, side_1, far_1))
        even = dev_index % 2 == 0
        table = jnp.stack([jnp.where(even, table, table_side), jnp.where(even, table_side, table)])
        lines = [list(range(y, dev_count, 2)) for y in range(2)]
        table = lax.all_gather(table[None], "expert", axis_index_groups=lines, tiled=True)
        table = table.reshape(dev_count, *table.shape[2:])

        moved_pair, last, side_2, far_2 = gate(
            (moved_pair, last, side_2, far_2), (diag_1, set_a[2])
        )
        third = jnp.where(inner, moved_pair, last)
        side_3, far_3 = from_peer(third, 1), from_plane(third, 1)
        order_b = ((1, 1), (1, 3), (1, 4), (0, 5), (0, 6))
        set_b = project(order_b, (diag_0, diag_1, far_2, side_2, third))
        top_2 = from_peer(far_2[:middle], 1)
        low_2 = from_plane(side_2[middle:], 1)

        side_3, far_3 = gate((side_3, far_3), (top_2, low_2, set_b[2]))
        top_3 = from_peer(far_3[:middle], 1)
        low_3 = from_plane(side_3[middle:], 1)
        order_d = ((1, 6), (0, 7), (1, 5), (1, 7))
        pieces = (far_3, side_3, top_2, low_2, top_3, low_3)

        sources = [*order_a, *order_b, *order_d]
        at_planes = jnp.array([p for p, _ in sources], jnp.int32)
        at_peers = peers[jnp.array([k for _, k in sources], jnp.int32)]
        (places,) = gate((jnp.stack([at_planes, at_peers], axis=1),), (set_b[2],))
        scaled = scaled_rows(places, own_expert, scales, rows, table)
        early = early_grad([set_a[3], set_b[3]], scaled)
        early = early.reshape(slot_dev, CORES, shard_rows, feature_count)
        scaled = scaled.reshape(slot_dev, CORES, shard_rows, -1)
        (given,) = last_grad(1 - core_at, pieces, scaled, early)
        given = from_sibling(given)
        set_d = project(order_d, pieces, keep=False)
        state = last_grad(
            core_at, pieces, scaled, early, (given, master, first_moment, second_moment)
        )

        sets = (set_a, set_b, set_d)
        far_backs = [from_plane(s[1], 1) for s in sets]
        hidden_grad = hidden_parts(
            peers,
            plane_at,
            [s[0] for s in sets],
            far_backs,
            state[1],
            [k for p, k in sources if p == 0],
            [k for p, k in sources if p == 1],
        )
        sums = jnp.concatenate([s[2] for s in sets], axis=1)
        ranks = [[sources.index((p, k)) for k in range(dev_count)] for p in range(planes)]
        sums = sums[:, jnp.array(ranks, jnp.int32)[:, position]].transpose(1, 2, 0, 3)
        sums = jnp.stack(by_plane([sums[0], sums[1]])).reshape(-1, slot_dev, tok_rows)
        cores = [
            [(x * CORES + c) * dev_count + d for x in range(planes) for d in range(dev_count)]
            for c in range(CORES)
        ]
        sums = lax.all_to_all(
            sums, ("dp", "expert"), 0, 0, axis_index_groups=cores, tiled=True
        )
        sums = add_planes(sums, state[1]).transpose(0, 2, 1)
        return finish(hidden_grad, sums, state)

    hidden = saved_hidden[0, 0].reshape(dev_count, slot_dev, capacity, planes, plane_rows)

    def hidden_for(shift):
        at = (plane + shift) % planes
        return lax.dynamic_index_in_dim(hidden, at, 3, keepdims=False)

    rows = [hidden_for(0)] + [from_plane(hidden_for(i), i) for i in range(1, planes)]

    own_weight = master.astype(bf16)
    other_weight = from_sibling(own_weight)
    weight = jnp.stack([own_weight, other_weight], axis=1)
    weight = jnp.where(core == 0, weight, weight[:, ::-1]).reshape(width, feature_count)
    before = (jnp.arange(tok_rows)[:, None] > jnp.arange(tok_rows)[None, :]).astype(bf16)
    places = jnp.arange(capacity, dtype=jnp.int32)
    gates = matmul("xqts,sk->xqkt", all_gates, columns)
    live = gates > 0
    spot = matmul("ut,xqkt->xqku", before, live.astype(bf16)).astype(jnp.int32)
    hits = (live[..., None, :] & (spot[..., None, :] == places[:, None])).astype(bf16)
    gates = gates[:, :, : 2 * slot_dev].astype(bf16)

    moved = matmul("xqjat,xqlct->xqjalc", hits[:, :, 2 * slot_dev :], hits[:, :, :slot_dev])
    moved = moved.astype(bf16) * hot_own.T[None, None, :, None, :, None]
    moved = [moved[i] for i in range(planes)]
    hot_rows = [
        matmul("qjalc,qlch->qjah", a, b).astype(bf16) for a, b in zip(moved, by_plane(rows))
    ]
    hot_rows = lax.psum(jnp.stack(hot_rows), "expert")

    def expert_rows(shift, own):
        table = lax.dynamic_index_in_dim(hot_rows, (plane - shift) % planes, 0, keepdims=False)
        picked = own
        for j in range(HOT):
            picked = jnp.where((own_expert == j)[None, :, None, None], table[:, j, None], picked)
        return picked

    def project(tokens, source_gates, source_hits, own):
        count = source_hits.shape[0]
        projected = matmul("td,hd->th", tokens, weight)
        projected = projected.reshape(count, tok_rows, slot_dev, plane_rows)
        slot_hits = source_hits[:, :slot_dev]
        spread = matmul("qlct,qlch->qtlh", slot_hits, own)
        gate_sums = jnp.sum(spread * projected, axis=3)
        scatter = slot_hits * source_gates[:, :slot_dev, None, :]
        back = matmul("qlct,qtlh->qlch", scatter, projected.astype(bf16)).astype(bf16)
        return gate_sums, back

    def scale(source_gates, source_hits, expert_own):
        count = source_hits.shape[0]
        scatter = source_hits[:, slot_dev : 2 * slot_dev] * source_gates[:, slot_dev:, None, :]
        scaled = matmul("qlct,qlch->qtlh", scatter, expert_own).astype(bf16)
        return scaled.reshape(count * tok_rows, width)

    def step(carry, at):
        tokens, total = carry
        shift, own = at
        gathered = lax.all_gather(tokens, "expert", tiled=True)
        source = (plane - shift) % planes
        source_gates = lax.dynamic_index_in_dim(gates, source, 0, keepdims=False)
        source_hits = lax.dynamic_index_in_dim(hits, source, 0, keepdims=False)
        sums, back = project(gathered, source_gates, source_hits, own)
        scaled = scale(source_gates, source_hits, expert_rows(shift, own))
        total = total + matmul("th,td->hd", scaled, gathered)
        return (from_plane(tokens, 1), total), (sums, back)

    start = (grad_out, jnp.zeros((width, feature_count), f32))
    (_, grads), (sums, backs) = lax.scan(step, start, (jnp.arange(planes), jnp.stack(rows)))

    backs = [backs[0]] + [from_plane(backs[i], -i) for i in range(1, planes)]
    order = (jnp.arange(planes) - plane) % planes
    hidden_grad = jnp.concatenate(list(jnp.take(jnp.stack(backs), order, axis=0)), axis=-1)
    gate_sums = sums[0]
    for i in range(1, planes):
        gate_sums = gate_sums + from_plane(sums[i], -i)

    grads = grads.reshape(slot_dev, CORES, shard_rows, feature_count)
    kept = lax.dynamic_index_in_dim(grads, core, 1, keepdims=False)
    given = lax.dynamic_index_in_dim(grads, 1 - core, 1, keepdims=False)
    grad_total = kept + from_sibling(given.astype(bf16)).astype(f32)
    state = adam(grad_total, master, first_moment, second_moment)
    gate_sums = lax.all_to_all(gate_sums, "expert", split_axis=0, concat_axis=0, tiled=True)
    return finish(hidden_grad, gate_sums, state)


def solution(mesh):
    placed = (
        P(("dp", "expert"), None),
        P(("dp", "expert"), None),
        P(("dp", "expert"), None),
        P(("dp", "expert"), None),
        P(),
        P("dp", "expert", None, None, None, None),
        P("expert", "dp", None),
        P("expert", "dp", None),
        P("expert", "dp", None),
    )
    return jax.shard_map(
        on_device,
        mesh=mesh,
        in_specs=placed,
        out_specs=(
            P("dp", "expert", None, None, None, None),
            P(("dp", "expert"), None),
            P("expert", "dp", None),
            P("expert", "dp", None),
            P("expert", "dp", None),
        ),
        check_vma=False,
    )
```
